32 devices in a mesh: clu: 8 (over y, x, core), mem: 4 (over z).
Axes of the slice: x: 2, y: 2, z: 4, core: 2. Of those that a mesh axis runs over, the one named last changes fastest.
Arguments:
- seed_class: int32 [8192], P(('clu', 'mem')), may hold values from 0 to 15
- seed_weight: float32 [8192], P(('clu', 'mem')), may hold values from 0.3 to 3
- tile_values: bfloat16 [8, 4, 96, 128, 128], P('clu', 'mem'), may hold values from 0 to 1
- tile_rows: int32 [8, 4, 96], P('clu', 'mem'), may hold values from 0 to 7
- tile_cols: int32 [8, 4, 96], P('clu', 'mem'), may hold values from 0 to 15
- tile_count: int32 [8, 4], P('clu', 'mem'), may hold values from 12 to 96, as said below
Outputs:
- scores: float32 [8, 8192], P(None, ('clu', 'mem'))
- residual: float32 [8, 8192], P(None, ('clu', 'mem'))
The draws below stay inside these ranges and needn't reach their ends.
Inputs may be any that keep to these rules, and one draw needn't show every extreme that they name: `tile_count`: some device uses all 96 slots in every draw.
All inputs are finite; a program needn't handle non-finite values.
Results may differ from the reference program's by a relative error of at most 0.0027.
Values may be sent and summed in bfloat16 or wider, within the bound.
A program may use at most 64 MiB of HBM per device.

```python
import math
import jax
import jax.numpy as jnp
from jax import lax

TILE = 128
CLASSES = 8
NB_DEV = 2
TCAP = 96
ITERS = 2
NODES = 8192
RB = 8
CB = 16
N_CLU = 8
N_MEM = 4


def draw_tile_count(key, part):
    key = jax.random.fold_in(key, 11)
    first, second = jax.random.split(key)
    total = N_CLU * N_MEM
    lowest = max(TCAP // 8, 1)
    counts = jax.random.randint(first, (total,), lowest, TCAP + 1)
    heavy = jax.random.randint(second, (), 0, total)
    counts = jnp.where(jnp.arange(total) == heavy, TCAP, counts)
    return counts.reshape(N_CLU, N_MEM).astype(jnp.int32)


def sparse_tiles(key, lowest):
    first, second = jax.random.split(key)
    shape = (N_CLU, N_MEM, TCAP, TILE, TILE)
    keep = min(0.9, 56.0 / (TCAP // NB_DEV * TILE))
    kept = jax.random.bernoulli(first, keep, shape).astype(jnp.float32)
    values = jax.random.uniform(second, shape, jnp.float32, lowest, 1.0)
    return (kept * values).astype(jnp.bfloat16)


def draw_tile_values(key, part):
    key = jax.random.fold_in(key, 23)
    return sparse_tiles(key, 0.1)


def touch_ends(result, own_key, smallest, top_value):
    extent = result.shape
    index_at = [jax.random.randint(jax.random.fold_in(own_key, axis), (), 0, extent[axis]) for axis in range(len(extent))]
    result = result.at[tuple(index_at)].set(smallest)
    longest = extent.index(max(extent))
    index_at[longest] = (index_at[longest] + 1) % extent[longest]
    return result.at[tuple(index_at)].set(top_value)


def level_of(rng, extent, cuts, least, largest):
    factor_of, own = 1.0, jax.random.fold_in(rng, 6)
    for dim, blocks in cuts:
        draws = jnp.exp(jax.random.uniform(jax.random.fold_in(own, dim), (blocks,), jnp.float32, least / len(cuts), largest / len(cuts)))
        factor_of = factor_of * jnp.repeat(draws, extent[dim] // blocks).reshape([-1 if axis == dim else 1 for axis in range(len(extent))])
    return factor_of


def setup_inputs(seed: int = 0) -> dict:
    key_list = jax.random.split(jax.random.key(seed), 7)
    seed_class = touch_ends(jax.random.randint(key_list[0], (NODES,), 0, 2 * CLASSES), jax.random.fold_in(key_list[0], 1), 0, (2 * CLASSES) - 1).astype(jnp.int32)
    seed_weight = jnp.clip(jnp.exp(math.log(3.0) - 2.3025851 * jax.random.uniform(key_list[1], (NODES,), jnp.float32) ** level_of(key_list[1], (NODES,), ((0, 32),), -0.2, 0.2)), 0.3, 3.0)
    tile_values = draw_tile_values(jax.random.fold_in(key_list[6], 71), 0)
    tile_rows = touch_ends(jax.random.randint(key_list[3], (N_CLU, N_MEM, TCAP), 0, RB), jax.random.fold_in(key_list[3], 1), 0, RB - 1).astype(jnp.int32)
    tile_cols = touch_ends(jax.random.randint(key_list[4], (N_CLU, N_MEM, TCAP), 0, CB), jax.random.fold_in(key_list[4], 1), 0, CB - 1).astype(jnp.int32)
    tile_count = draw_tile_count(jax.random.fold_in(key_list[6], 71), 0)
    return dict(seed_class=seed_class, seed_weight=seed_weight, tile_values=tile_values, tile_rows=tile_rows, tile_cols=tile_cols, tile_count=tile_count)


def layout(tile_rows, tile_cols, tile_count):
    valid = (jnp.arange(TCAP, dtype=jnp.int32)[None, None, :] < tile_count[:, :, None]).astype(jnp.float32)
    global_rows = (jnp.arange(N_CLU, dtype=jnp.int32)[:, None, None] * RB + tile_rows).astype(jnp.int32)
    member = jnp.arange(N_MEM, dtype=jnp.int32)[None, :, None]
    global_cols = ((tile_cols // NB_DEV * N_MEM + member) * NB_DEV + tile_cols % NB_DEV).astype(jnp.int32)
    return (valid, global_rows, global_cols)

def reference(seed_class, seed_weight, tile_values, tile_rows, tile_cols, tile_count):
    blocks = NODES // TILE
    valid, global_rows, global_cols = layout(tile_rows, tile_cols, tile_count)

    def degree_step(carry, index):
        tiles_now = tile_values[index].astype(jnp.float32)
        mask = valid[index][:, :, None]
        row_part = lax.optimization_barrier(jnp.sum(tiles_now, axis=3)) * mask
        col_part = lax.optimization_barrier(jnp.sum(tiles_now, axis=2)) * mask
        carry = carry.at[global_rows[index]].add(row_part)
        carry = carry.at[global_cols[index]].add(col_part)
        return (carry, None)
    start = jnp.zeros((blocks, TILE), jnp.float32)
    summed, _ = lax.scan(degree_step, start, jnp.arange(N_CLU, dtype=jnp.int32))
    degree = 1.0 + summed.reshape(NODES)
    inverse_root = lax.rsqrt(degree)

    def operate(panel):
        scaled = lax.optimization_barrier((inverse_root[None, :] * panel).astype(jnp.bfloat16)).astype(jnp.float32)
        blocked = jnp.transpose(scaled.reshape(CLASSES, blocks, TILE), (1, 0, 2))

        def apply_step(carry, index):
            tiles_now = tile_values[index].astype(jnp.float32)
            mask = valid[index][:, :, None, None]
            from_cols = blocked[global_cols[index]]
            forward = jnp.einsum('mtij,mtcj->mtci', tiles_now, from_cols) * mask
            from_rows = blocked[global_rows[index]]
            backward = jnp.einsum('mtij,mtci->mtcj', tiles_now, from_rows) * mask
            carry = carry.at[global_rows[index]].add(forward)
            carry = carry.at[global_cols[index]].add(backward)
            return (carry, None)
        start_sum = jnp.zeros((blocks, CLASSES, TILE), jnp.float32)
        image_sum, _ = lax.scan(apply_step, start_sum, jnp.arange(N_CLU, dtype=jnp.int32))
        image_sum = jnp.transpose(image_sum, (1, 0, 2)).reshape(CLASSES, NODES)
        return panel - 0.99 * inverse_root[None, :] * image_sum
    classes_now = jnp.arange(CLASSES, dtype=jnp.int32)[:, None]
    labels = jnp.where(seed_class[None, :] == classes_now, seed_weight[None, :], jnp.float32(0.0)).astype(jnp.float32)
    scores = jnp.zeros_like(labels)
    residual = labels
    direction = labels
    norm_now = lax.optimization_barrier(jnp.sum(residual * residual, axis=1))
    for step in range(ITERS):
        image = operate(direction)
        alpha = norm_now / lax.optimization_barrier(jnp.sum(direction * image, axis=1))
        scores = scores + alpha[:, None] * direction
        residual = residual - alpha[:, None] * image
        if step + 1 < ITERS:
            norm_next = lax.optimization_barrier(jnp.sum(residual * residual, axis=1))
            direction = residual + (norm_next / norm_now)[:, None] * direction
            norm_now = norm_next
    return (scores, residual)
```

```python
import functools
import jax
import jax.numpy as jnp
from jax import lax
from jax.experimental import pallas as pl
from jax.experimental.pallas import tpu as pltpu
from jax.sharding import PartitionSpec as P

CLASSES = 8
NB_DEV = 2
ITERS = 2
CHUNKS = 4
DENSE_LIMIT = 16 * 1024 * 1024
MESH = pl.DeviceIdType.MESH


def spread(row_part, col_part):
    width = row_part.shape[0]
    from_rows = lax.psum_scatter(
        row_part.reshape(width, -1), "mem", scatter_dimension=1, tiled=True
    )
    from_cols = lax.psum_scatter(
        col_part.reshape(width, -1), "clu", scatter_dimension=1, tiled=True
    )
    return from_rows + from_cols


def squares(residual):
    return lax.psum(jnp.sum(residual * residual, axis=1), ("clu", "mem"))


def on_device_slots(seed_class, seed_weight, tile_values, tile_rows, tile_cols, tile_count):
    tiles = tile_values[0, 0]
    rows = tile_rows[0, 0]
    cols = tile_cols[0, 0]
    count = tile_count[0, 0]
    slots = tiles.shape[0]
    side = tiles.shape[1]
    row_blocks = NB_DEV * lax.axis_size("mem")
    col_blocks = NB_DEV * lax.axis_size("clu")
    valid = (jnp.arange(slots, dtype=jnp.int32) < count).astype(jnp.float32)
    row_table = (rows[None, :] == jnp.arange(row_blocks, dtype=jnp.int32)[:, None]).astype(
        jnp.float32
    ) * valid[None, :]
    col_table = (cols[None, :] == jnp.arange(col_blocks, dtype=jnp.int32)[:, None]).astype(
        jnp.float32
    ) * valid[None, :]
    highest = lax.Precision.HIGHEST
    row_totals = jnp.sum(tiles, axis=2, dtype=jnp.float32)
    col_totals = jnp.sum(tiles, axis=1, dtype=jnp.float32)
    row_part = jnp.einsum("rt,ti->ri", row_table, row_totals, precision=highest)
    col_part = jnp.einsum("kt,tj->kj", col_table, col_totals, precision=highest)
    degree = 1.0 + spread(row_part[None], col_part[None])[0]
    inverse_root = lax.rsqrt(degree)
    classes_now = jnp.arange(CLASSES, dtype=jnp.int32)[:, None]
    labels = jnp.where(seed_class[None, :] == classes_now, seed_weight[None, :], jnp.float32(0.0))
    scores = jnp.zeros_like(labels)
    residual = labels
    direction = labels
    norm_now = squares(residual)
    for step in range(ITERS):
        width = direction.shape[0]
        scaled = (inverse_root[None, :] * direction).astype(jnp.bfloat16)
        col_panel = lax.all_gather(scaled, "clu", axis=1, tiled=True).reshape(
            width, col_blocks, side
        )
        row_panel = lax.all_gather(scaled, "mem", axis=1, tiled=True).reshape(
            width, row_blocks, side
        )
        forward = jnp.einsum(
            "tij,ctj->cti",
            tiles,
            jnp.take(col_panel, cols, axis=1),
            preferred_element_type=jnp.float32,
        )
        backward = jnp.einsum(
            "tij,cti->ctj",
            tiles,
            jnp.take(row_panel, rows, axis=1),
            preferred_element_type=jnp.float32,
        )
        row_sum = jnp.einsum("rt,cti->cri", row_table, forward, precision=highest)
        col_sum = jnp.einsum("kt,ctj->ckj", col_table, backward, precision=highest)
        image_sum = spread(row_sum, col_sum)
        image = direction - 0.99 * inverse_root[None, :] * image_sum
        alpha = norm_now / lax.psum(jnp.sum(direction * image, axis=1), ("clu", "mem"))
        scores = scores + alpha[:, None] * direction
        residual = residual - alpha[:, None] * image
        if step + 1 < ITERS:
            norm_next = squares(residual)
            direction = residual + (norm_next / norm_now)[:, None] * direction
            norm_now = norm_next
    return (scores, residual)


def densify_kernel(
    rows_ref, cols_ref, count_ref, tiles_hbm, w_ref, row_ref, col_ref, tiles, dense, sems
):
    slots, side, _ = tiles.shape
    row_blocks = w_ref.shape[0] // side
    col_blocks = w_ref.shape[1] // side
    chunk = slots // CHUNKS
    copies = [
        pltpu.make_async_copy(
            tiles_hbm.at[pl.ds(k * chunk, chunk)], tiles.at[pl.ds(k * chunk, chunk)], sems.at[k]
        )
        for k in range(CHUNKS)
    ]
    for copy in copies:
        copy.start()

    def clear(k, carry):
        dense[k] = jnp.zeros((side, side), jnp.float32)
        return carry

    lax.fori_loop(0, row_blocks * col_blocks, clear, 0)
    count = count_ref[0]

    def add(s, carry):
        place = rows_ref[s] * col_blocks + cols_ref[s]
        dense[place] += tiles[s].astype(jnp.float32)
        return carry

    for k in range(CHUNKS):
        copies[k].wait()
        lax.fori_loop(k * chunk, jnp.clip(count, k * chunk, (k + 1) * chunk), add, 0)

    col_sums = [jnp.zeros((8, side), jnp.float32) for _ in range(col_blocks)]
    for r in range(row_blocks):
        row_sum = jnp.zeros((side, side), jnp.float32)
        for c in range(col_blocks):
            block = dense[r * col_blocks + c]
            w_ref[r * side : (r + 1) * side, c * side : (c + 1) * side] = block.astype(jnp.bfloat16)
            row_sum = row_sum + block
            col_sums[c] = col_sums[c] + jnp.sum(block.reshape(side // 8, 8, side), axis=0)
        at = (r % NB_DEV) * side
        row_ref[r // NB_DEV, :, at : at + side] = jnp.sum(row_sum.T, axis=0, keepdims=True)
    for c in range(col_blocks):
        at = (c % NB_DEV) * side
        col_ref[c // NB_DEV, :, at : at + side] = jnp.sum(col_sums[c], axis=0, keepdims=True)


def split(panel):
    high = panel.astype(jnp.bfloat16)
    low = (panel - high.astype(jnp.float32)).astype(jnp.bfloat16)
    return jnp.concatenate([high, low], axis=0)


def solve_kernel(
    n_clu,
    n_mem,
    class_ref,
    weight_ref,
    w_hbm,
    row_ref,
    col_ref,
    scores_ref,
    residual_ref,
    w,
    deg_m,
    deg_c,
    own,
    pan_m,
    pan_c,
    part_m,
    part_c,
    got_m,
    got_c,
    dots,
    got_dots,
    w_sem,
    send_m,
    recv_m,
    send_c,
    recv_c,
    send_d,
    recv_d,
):
    me_c = lax.axis_index("clu")
    me_m = lax.axis_index("mem")
    total = n_clu * n_mem
    place = me_c * n_mem + me_m

    def member(k):
        other = lax.rem(place + k, total)
        return (lax.div(other, n_mem), lax.rem(other, n_mem))

    w_copy = pltpu.make_async_copy(w_hbm, w, w_sem)
    w_copy.start()
    barrier = pltpu.get_barrier_semaphore()

    def greet(k, carry):
        pl.semaphore_signal(barrier, inc=1, device_id=member(k), device_id_type=MESH)
        return carry

    lax.fori_loop(1, total, greet, 0)

    sent = []

    def over_mem(phase, source, target):
        copies = []
        for k in range(1, n_mem):
            other = lax.rem(me_m + k, n_mem)
            copies.append(
                pltpu.make_async_remote_copy(
                    src_ref=source(other),
                    dst_ref=target(k),
                    send_sem=send_m.at[phase, k],
                    recv_sem=recv_m.at[phase, k],
                    device_id=(me_c, other),
                    device_id_type=MESH,
                )
            )
            copies[-1].start()
        sent.extend(copies)
        return copies

    def over_clu(phase, source, target):
        copies = []
        for k in range(1, n_clu):
            other = lax.rem(me_c + k, n_clu)
            copies.append(
                pltpu.make_async_remote_copy(
                    src_ref=source(other),
                    dst_ref=target(k),
                    send_sem=send_c.at[phase, k],
                    recv_sem=recv_c.at[phase, k],
                    device_id=(other, me_m),
                    device_id_type=MESH,
                )
            )
            copies[-1].start()
        sent.extend(copies)
        return copies

    def arrive(copies):
        for copy in copies:
            copy.wait_recv()

    weight = weight_ref[...]
    kinds = lax.broadcasted_iota(jnp.int32, (CLASSES, weight.shape[1]), 0)
    labels = jnp.where(class_ref[...] == kinds, weight, jnp.float32(0.0))
    pl.semaphore_wait(barrier, total - 1)

    from_m = over_mem(0, lambda o: row_ref.at[o], lambda k: deg_m.at[k])
    from_c = over_clu(0, lambda o: col_ref.at[o], lambda k: deg_c.at[k])
    degree = 1.0 + (row_ref[me_m] + col_ref[me_c])
    arrive(from_m)
    for k in range(1, n_mem):
        degree = degree + deg_m[k]
    arrive(from_c)
    for k in range(1, n_clu):
        degree = degree + deg_c[k]
    root = lax.rsqrt(degree)

    def gather(step, panel):
        own[step] = panel
        pan_m[step, me_m] = panel
        pan_c[step, me_c] = panel
        from_m = over_mem(1 + 2 * step, lambda o: own.at[step], lambda k: pan_m.at[step, me_m])
        from_c = over_clu(1 + 2 * step, lambda o: own.at[step], lambda k: pan_c.at[step, me_c])
        return from_m, from_c

    def multiply(step, from_m, from_c, prepare):
        phase = 2 + 2 * step
        arrive(from_m)
        left = jnp.concatenate([pan_m[step, k] for k in range(n_mem)], axis=1)
        if step == 0:
            w_copy.wait()
        out = lax.dot_general(
            prepare(left), w[...], (((1,), (0,)), ((), ())), preferred_element_type=jnp.float32
        )
        out = out[:CLASSES] if step == 0 else out[:CLASSES] + out[CLASSES:]
        width = out.shape[1] // n_clu
        for k in range(n_clu):
            part_c[step, k] = out[:, k * width : (k + 1) * width]
        back_c = over_clu(phase, lambda o: part_c.at[step, o], lambda k: got_c.at[step, k])
        arrive(from_c)
        right = jnp.concatenate([pan_c[step, k] for k in range(n_clu)], axis=1)
        out = lax.dot_general(
            prepare(right), w[...], (((1,), (1,)), ((), ())), preferred_element_type=jnp.float32
        )
        out = out[:CLASSES] if step == 0 else out[:CLASSES] + out[CLASSES:]
        for k in range(n_mem):
            part_m[step, k] = out[:, k * width : (k + 1) * width]
        back_m = over_mem(phase, lambda o: part_m.at[step, o], lambda k: got_m.at[step, k])
        return back_m, back_c, jnp.sum(left * out, axis=1, keepdims=True)

    def collect(step, back_m, back_c):
        image = part_m[step, me_m] + part_c[step, me_c]
        arrive(back_c)
        for k in range(1, n_clu):
            image = image + got_c[step, k]
        arrive(back_m)
        for k in range(1, n_mem):
            image = image + got_m[step, k]
        return 0.99 * root * image

    from_m, from_c = gather(0, root * labels)
    back_m, back_c, _ = multiply(0, from_m, from_c, lambda x: x.astype(jnp.bfloat16))
    first = collect(0, back_m, back_c)

    from_m, from_c = gather(1, root * first)
    sums = [
        jnp.sum(labels * labels, axis=1, keepdims=True),
        jnp.sum(labels * first, axis=1, keepdims=True),
        jnp.sum(first * first, axis=1, keepdims=True),
    ]
    back_m, back_c, cross = multiply(1, from_m, from_c, split)
    sums.append(1.98 * cross)

    lane = lax.broadcasted_iota(jnp.int32, (CLASSES, 128), 1)
    kind = lax.broadcasted_iota(jnp.int32, (CLASSES, 128), 0)
    line = jnp.zeros((CLASSES, 128), jnp.float32)
    for k, value in enumerate(sums):
        line = line + jnp.where(lane == kind + k * CLASSES, value, 0.0)
    line = jnp.sum(line, axis=0, keepdims=True)
    dots[...] = line

    def dot_copy(k):
        return pltpu.make_async_remote_copy(
            src_ref=dots,
            dst_ref=got_dots.at[k],
            send_sem=send_d.at[k],
            recv_sem=recv_d.at[k],
            device_id=member(k),
            device_id_type=MESH,
        )

    def send_dot(k, carry):
        dot_copy(k).start()
        return carry

    def take_dot(k, carry):
        dot_copy(k).wait_recv()
        return carry + got_dots[k]

    lax.fori_loop(1, total, send_dot, 0)
    second = collect(1, back_m, back_c)
    line = lax.fori_loop(1, total, take_dot, line)
    spread_line = jnp.broadcast_to(line, (CLASSES, 128))
    bb, bq, qq, qt = [
        jnp.sum(
            jnp.where(lane == kind + k * CLASSES, spread_line, 0.0), axis=1, keepdims=True
        )
        for k in range(4)
    ]
    alpha = bb / (bb - bq)
    ratio = bq / bb
    norm = alpha * alpha * (qq - ratio * bq)
    beta = norm / bb
    h = beta - alpha * ratio
    curve = alpha * alpha * (qq - qt) + 2.0 * alpha * h * (bq - qq) + h * h * (bb - bq)
    alpha_next = norm / curve
    direction = alpha * first + h * labels
    image = alpha * (first - second) + h * (labels - first)
    scores_ref[...] = alpha * labels + alpha_next * direction
    residual_ref[...] = alpha * (first - ratio * labels) - alpha_next * image

    def leave_dot(k, carry):
        dot_copy(k).wait_send()
        return carry

    lax.fori_loop(1, total, leave_dot, 0)
    for copy in sent:
        copy.wait_send()


def on_device_dense(seed_class, seed_weight, tile_values, tile_rows, tile_cols, tile_count):
    n_clu = lax.axis_size("clu")
    n_mem = lax.axis_size("mem")
    tiles = tile_values[0, 0]
    slots, side, _ = tiles.shape
    nodes = NB_DEV * side
    rows = nodes * n_mem
    cols = nodes * n_clu
    f32 = jnp.float32
    smem = pl.BlockSpec(memory_space=pltpu.SMEM)
    vmem = pl.BlockSpec(memory_space=pltpu.VMEM)
    hbm = pl.BlockSpec(memory_space=pl.ANY)
    w, row_total, col_total = pl.pallas_call(
        densify_kernel,
        out_shape=(
            jax.ShapeDtypeStruct((rows, cols), jnp.bfloat16),
            jax.ShapeDtypeStruct((n_mem, 1, nodes), f32),
            jax.ShapeDtypeStruct((n_clu, 1, nodes), f32),
        ),
        in_specs=[smem, smem, smem, hbm],
        out_specs=(vmem, vmem, vmem),
        scratch_shapes=[
            pltpu.VMEM((slots, side, side), tiles.dtype),
            pltpu.VMEM((rows * cols // (side * side), side, side), f32),
            pltpu.SemaphoreType.DMA((CHUNKS,)),
        ],
        compiler_params=pltpu.CompilerParams(vmem_limit_bytes=24 * 1024 * 1024),
        name="densify",
    )(tile_rows[0, 0], tile_cols[0, 0], tile_count[0], tiles)
    panel = (CLASSES, nodes)
    dma = pltpu.SemaphoreType.DMA
    return pl.pallas_call(
        functools.partial(solve_kernel, n_clu, n_mem),
        out_shape=(jax.ShapeDtypeStruct(panel, f32), jax.ShapeDtypeStruct(panel, f32)),
        in_specs=[vmem, vmem, hbm, vmem, vmem],
        out_specs=(vmem, vmem),
        scratch_shapes=[
            pltpu.VMEM((rows, cols), jnp.bfloat16),
            pltpu.VMEM((n_mem, 1, nodes), f32),
            pltpu.VMEM((n_clu, 1, nodes), f32),
            pltpu.VMEM((ITERS, *panel), f32),
            pltpu.VMEM((ITERS, n_mem, *panel), f32),
            pltpu.VMEM((ITERS, n_clu, *panel), f32),
            pltpu.VMEM((ITERS, n_mem, *panel), f32),
            pltpu.VMEM((ITERS, n_clu, *panel), f32),
            pltpu.VMEM((ITERS, n_mem, *panel), f32),
            pltpu.VMEM((ITERS, n_clu, *panel), f32),
            pltpu.VMEM((1, 128), f32),
            pltpu.VMEM((n_clu * n_mem, 1, 128), f32),
            dma,
            dma((1 + 2 * ITERS, n_mem)),
            dma((1 + 2 * ITERS, n_mem)),
            dma((1 + 2 * ITERS, n_clu)),
            dma((1 + 2 * ITERS, n_clu)),
            dma((n_clu * n_mem,)),
            dma((n_clu * n_mem,)),
        ],
        compiler_params=pltpu.CompilerParams(
            collective_id=0, has_side_effects=True, vmem_limit_bytes=16 * 1024 * 1024
        ),
        name="solve",
    )(seed_class[None], seed_weight[None], w, row_total, col_total)


def on_device(seed_class, seed_weight, tile_values, tile_rows, tile_cols, tile_count):
    side = tile_values.shape[-1]
    blocks = NB_DEV * lax.axis_size("mem") * NB_DEV * lax.axis_size("clu")
    if blocks * side * side * 4 <= DENSE_LIMIT:
        run = on_device_dense
    else:
        run = on_device_slots
    return run(seed_class, seed_weight, tile_values, tile_rows, tile_cols, tile_count)


def solution(mesh):
    in_specs = (
        P(("clu", "mem")),
        P(("clu", "mem")),
        P("clu", "mem", None, None, None),
        P("clu", "mem", None),
        P("clu", "mem", None),
        P("clu", "mem"),
    )
    out_specs = (P(None, ("clu", "mem")), P(None, ("clu", "mem")))
    return jax.shard_map(
        on_device, mesh=mesh, in_specs=in_specs, out_specs=out_specs, check_vma=False
    )
```

```python
import functools
import jax
import jax.numpy as jnp
from jax import lax
from jax.experimental import pallas as pl
from jax.experimental.pallas import tpu as pltpu
from jax.sharding import PartitionSpec as P

CLASSES = 8
NB_DEV = 2
ITERS = 2
CHUNKS = 4
DENSE_LIMIT = 16 * 1024 * 1024
VMEM_LIMIT = 64 * 1024 * 1024
MESH = pl.DeviceIdType.MESH


def spread(row_part, col_part):
    width = row_part.shape[0]
    from_rows = lax.psum_scatter(
        row_part.reshape(width, -1), "mem", scatter_dimension=1, tiled=True
    )
    from_cols = lax.psum_scatter(
        col_part.reshape(width, -1), "clu", scatter_dimension=1, tiled=True
    )
    return from_rows + from_cols


def squares(residual):
    return lax.psum(jnp.sum(residual * residual, axis=1), ("clu", "mem"))


def on_device_slots(seed_class, seed_weight, tile_values, tile_rows, tile_cols, tile_count):
    tiles = tile_values[0, 0]
    rows = tile_rows[0, 0]
    cols = tile_cols[0, 0]
    count = tile_count[0, 0]
    slots = tiles.shape[0]
    side = tiles.shape[1]
    row_blocks = NB_DEV * lax.axis_size("mem")
    col_blocks = NB_DEV * lax.axis_size("clu")
    valid = (jnp.arange(slots, dtype=jnp.int32) < count).astype(jnp.float32)
    row_table = (rows[None, :] == jnp.arange(row_blocks, dtype=jnp.int32)[:, None]).astype(
        jnp.float32
    ) * valid[None, :]
    col_table = (cols[None, :] == jnp.arange(col_blocks, dtype=jnp.int32)[:, None]).astype(
        jnp.float32
    ) * valid[None, :]
    highest = lax.Precision.HIGHEST
    row_totals = jnp.sum(tiles, axis=2, dtype=jnp.float32)
    col_totals = jnp.sum(tiles, axis=1, dtype=jnp.float32)
    row_part = jnp.einsum("rt,ti->ri", row_table, row_totals, precision=highest)
    col_part = jnp.einsum("kt,tj->kj", col_table, col_totals, precision=highest)
    degree = 1.0 + spread(row_part[None], col_part[None])[0]
    inverse_root = lax.rsqrt(degree)
    classes_now = jnp.arange(CLASSES, dtype=jnp.int32)[:, None]
    labels = jnp.where(seed_class[None, :] == classes_now, seed_weight[None, :], jnp.float32(0.0))
    scores = jnp.zeros_like(labels)
    residual = labels
    direction = labels
    norm_now = squares(residual)
    for step in range(ITERS):
        width = direction.shape[0]
        scaled = (inverse_root[None, :] * direction).astype(jnp.bfloat16)
        col_panel = lax.all_gather(scaled, "clu", axis=1, tiled=True).reshape(
            width, col_blocks, side
        )
        row_panel = lax.all_gather(scaled, "mem", axis=1, tiled=True).reshape(
            width, row_blocks, side
        )
        forward = jnp.einsum(
            "tij,ctj->cti",
            tiles,
            jnp.take(col_panel, cols, axis=1),
            preferred_element_type=jnp.float32,
        )
        backward = jnp.einsum(
            "tij,cti->ctj",
            tiles,
            jnp.take(row_panel, rows, axis=1),
            preferred_element_type=jnp.float32,
        )
        row_sum = jnp.einsum("rt,cti->cri", row_table, forward, precision=highest)
        col_sum = jnp.einsum("kt,ctj->ckj", col_table, backward, precision=highest)
        image_sum = spread(row_sum, col_sum)
        image = direction - 0.99 * inverse_root[None, :] * image_sum
        alpha = norm_now / lax.psum(jnp.sum(direction * image, axis=1), ("clu", "mem"))
        scores = scores + alpha[:, None] * direction
        residual = residual - alpha[:, None] * image
        if step + 1 < ITERS:
            norm_next = squares(residual)
            direction = residual + (norm_next / norm_now)[:, None] * direction
            norm_now = norm_next
    return (scores, residual)


def densify_kernel(
    rows_hbm,
    cols_hbm,
    count_hbm,
    tiles_hbm,
    w_hbm,
    row_hbm,
    col_hbm,
    w_ref,
    row_ref,
    col_ref,
    rows_ref,
    cols_ref,
    count_ref,
    tiles,
    dense,
    small_sems,
    sems,
    out_sems,
):
    slots, side, _ = tiles.shape
    row_blocks = w_ref.shape[0] // side
    col_blocks = w_ref.shape[1] // side
    chunk = slots // CHUNKS
    small = [
        pltpu.make_async_copy(rows_hbm, rows_ref, small_sems.at[0]),
        pltpu.make_async_copy(cols_hbm, cols_ref, small_sems.at[1]),
        pltpu.make_async_copy(count_hbm, count_ref, small_sems.at[2]),
    ]
    for copy in small:
        copy.start()
    copies = [
        pltpu.make_async_copy(
            tiles_hbm.at[0, 0, pl.ds(k * chunk, chunk)], tiles.at[pl.ds(k * chunk, chunk)], sems.at[k]
        )
        for k in range(CHUNKS)
    ]
    for copy in copies:
        copy.start()

    def clear(k, carry):
        dense[k] = jnp.zeros((side, side), jnp.float32)
        return carry

    lax.fori_loop(0, row_blocks * col_blocks, clear, 0)
    for copy in small:
        copy.wait()
    count = count_ref[0, 0]

    def add(s, carry):
        place = rows_ref[0, 0, s] * col_blocks + cols_ref[0, 0, s]
        dense[place] += tiles[s].astype(jnp.float32)
        return carry

    for k in range(CHUNKS):
        copies[k].wait()
        lax.fori_loop(k * chunk, jnp.clip(count, k * chunk, (k + 1) * chunk), add, 0)

    results = []
    col_sums = [jnp.zeros((8, side), jnp.float32) for _ in range(col_blocks)]
    for r in range(row_blocks):
        row_sum = jnp.zeros((side, side), jnp.float32)
        for c in range(col_blocks):
            block = dense[r * col_blocks + c]
            w_ref[r * side : (r + 1) * side, c * side : (c + 1) * side] = block.astype(jnp.bfloat16)
            row_sum = row_sum + block
            col_sums[c] = col_sums[c] + jnp.sum(block.reshape(side // 8, 8, side), axis=0)
        at = (r % NB_DEV) * side
        row_ref[r // NB_DEV, :, at : at + side] = jnp.sum(row_sum.T, axis=0, keepdims=True)
        strip = pl.ds(r * side, side)
        results.append(pltpu.make_async_copy(w_ref.at[strip], w_hbm.at[strip], out_sems.at[r]))
        results[-1].start()
    for c in range(col_blocks):
        at = (c % NB_DEV) * side
        col_ref[c // NB_DEV, :, at : at + side] = jnp.sum(col_sums[c], axis=0, keepdims=True)
    results.append(pltpu.make_async_copy(row_ref, row_hbm, small_sems.at[0]))
    results.append(pltpu.make_async_copy(col_ref, col_hbm, small_sems.at[1]))
    for copy in results[-2:]:
        copy.start()
    for copy in results:
        copy.wait()


def split(panel):
    high = panel.astype(jnp.bfloat16)
    low = (panel - high.astype(jnp.float32)).astype(jnp.bfloat16)
    return jnp.concatenate([high, low], axis=0)


def solve_kernel(
    n_clu,
    n_mem,
    class_hbm,
    weight_hbm,
    w_hbm,
    row_hbm,
    col_hbm,
    scores_ref,
    residual_ref,
    class_ref,
    weight_ref,
    w,
    row_ref,
    col_ref,
    deg_m,
    deg_c,
    own,
    pan_m,
    pan_c,
    part_m,
    part_c,
    got_m,
    got_c,
    dots,
    dots_m,
    dots_c,
    load_sems,
    send_m,
    recv_m,
    send_c,
    recv_c,
):
    me_c = lax.axis_index("clu")
    me_m = lax.axis_index("mem")
    others_m = [None] + [lax.rem(me_m + k, n_mem) for k in range(1, n_mem)]
    others_c = [None] + [lax.rem(me_c + k, n_clu) for k in range(1, n_clu)]

    loads = [
        pltpu.make_async_copy(class_hbm, class_ref, load_sems.at[0]),
        pltpu.make_async_copy(weight_hbm, weight_ref, load_sems.at[1]),
        pltpu.make_async_copy(row_hbm, row_ref, load_sems.at[2]),
        pltpu.make_async_copy(col_hbm, col_ref, load_sems.at[3]),
    ]
    w_copy = pltpu.make_async_copy(w_hbm, w, load_sems.at[4])
    for copy in loads:
        copy.start()
    w_copy.start()
    barrier = pltpu.get_barrier_semaphore()
    for k in range(1, n_mem):
        pl.semaphore_signal(barrier, device_id=(me_c, others_m[k]), device_id_type=MESH)
    for k in range(1, n_clu):
        pl.semaphore_signal(barrier, device_id=(others_c[k], me_m), device_id_type=MESH)

    sent = []

    def over_mem(phase, source, target):
        copies = []
        for k in range(1, n_mem):
            copies.append(
                pltpu.make_async_remote_copy(
                    src_ref=source(others_m[k]),
                    dst_ref=target(k),
                    send_sem=send_m.at[phase, k],
                    recv_sem=recv_m.at[phase, k],
                    device_id=(me_c, others_m[k]),
                    device_id_type=MESH,
                )
            )
            copies[-1].start()
        sent.extend(copies)
        return copies

    def over_clu(phase, source, target):
        copies = []
        for k in range(1, n_clu):
            copies.append(
                pltpu.make_async_remote_copy(
                    src_ref=source(others_c[k]),
                    dst_ref=target(k),
                    send_sem=send_c.at[phase, k],
                    recv_sem=recv_c.at[phase, k],
                    device_id=(others_c[k], me_m),
                    device_id_type=MESH,
                )
            )
            copies[-1].start()
        sent.extend(copies)
        return copies

    def arrive(copies):
        for copy in copies:
            copy.wait_recv()

    for copy in loads:
        copy.wait()
    weight = weight_ref[...]
    kinds = lax.broadcasted_iota(jnp.int32, (CLASSES, weight.shape[1]), 0)
    labels = jnp.where(class_ref[...] == kinds, weight, jnp.float32(0.0))
    pl.semaphore_wait(barrier, n_mem + n_clu - 2)

    from_m = over_mem(0, lambda o: row_ref.at[o], lambda k: deg_m.at[k])
    from_c = over_clu(0, lambda o: col_ref.at[o], lambda k: deg_c.at[k])
    degree = 1.0 + (row_ref[me_m] + col_ref[me_c])
    arrive(from_m)
    for k in range(1, n_mem):
        degree = degree + deg_m[k]
    arrive(from_c)
    for k in range(1, n_clu):
        degree = degree + deg_c[k]
    root = lax.rsqrt(degree)

    def gather(step, panel):
        own[step] = panel
        pan_m[step, me_m] = panel
        pan_c[step, me_c] = panel
        from_m = over_mem(1 + 2 * step, lambda o: own.at[step], lambda k: pan_m.at[step, me_m])
        from_c = over_clu(1 + 2 * step, lambda o: own.at[step], lambda k: pan_c.at[step, me_c])
        return from_m, from_c

    def multiply(step, from_m, from_c, prepare, between):
        phase = 2 + 2 * step
        arrive(from_m)
        left = jnp.concatenate([pan_m[step, k] for k in range(n_mem)], axis=1)
        if step == 0:
            w_copy.wait()
        out = lax.dot_general(
            prepare(left), w[...], (((1,), (0,)), ((), ())), preferred_element_type=jnp.float32
        )
        out = out[:CLASSES] if step == 0 else out[:CLASSES] + out[CLASSES:]
        width = out.shape[1] // n_clu
        for k in range(n_clu):
            part_c[step, k] = out[:, k * width : (k + 1) * width]
        back_c = over_clu(phase, lambda o: part_c.at[step, o], lambda k: got_c.at[step, k])
        arrive(from_c)
        right = jnp.concatenate([pan_c[step, k] for k in range(n_clu)], axis=1)
        between(right, out)
        out = lax.dot_general(
            prepare(right), w[...], (((1,), (1,)), ((), ())), preferred_element_type=jnp.float32
        )
        out = out[:CLASSES] if step == 0 else out[:CLASSES] + out[CLASSES:]
        for k in range(n_mem):
            part_m[step, k] = out[:, k * width : (k + 1) * width]
        back_m = over_mem(phase, lambda o: part_m.at[step, o], lambda k: got_m.at[step, k])
        return back_m, back_c

    def collect(step, back_m, back_c):
        image = part_m[step, me_m] + part_c[step, me_c]
        arrive(back_c)
        for k in range(1, n_clu):
            image = image + got_c[step, k]
        arrive(back_m)
        for k in range(1, n_mem):
            image = image + got_m[step, k]
        return 0.99 * root * image

    from_m, from_c = gather(0, root * labels)
    back_m, back_c = multiply(
        0, from_m, from_c, lambda x: x.astype(jnp.bfloat16), lambda right, out: None
    )
    first = collect(0, back_m, back_c)

    from_m, from_c = gather(1, root * first)
    lane = lax.broadcasted_iota(jnp.int32, (CLASSES, 128), 1)
    kind = lax.broadcasted_iota(jnp.int32, (CLASSES, 128), 0)
    sums = [
        jnp.sum(labels * labels, axis=1, keepdims=True),
        jnp.sum(labels * first, axis=1, keepdims=True),
        jnp.sum(first * first, axis=1, keepdims=True),
    ]
    dot_copies = []

    def send_sums(right, image):
        cross = 1.98 * jnp.sum(right * image, axis=1, keepdims=True)
        line = jnp.zeros((CLASSES, 128), jnp.float32)
        for k, value in enumerate([*sums, cross]):
            line = line + jnp.where(lane == kind + k * CLASSES, value, 0.0)
        dots[0] = jnp.sum(line, axis=0, keepdims=True)
        dot_copies.extend(over_mem(5, lambda o: dots.at[0], lambda k: dots_m.at[k]))

    back_m, back_c = multiply(1, from_m, from_c, split, send_sums)
    arrive(dot_copies)
    line = dots[0]
    for k in range(1, n_mem):
        line = line + dots_m[k]
    dots[1] = line
    dot_copies = over_clu(5, lambda o: dots.at[1], lambda k: dots_c.at[k])
    second = collect(1, back_m, back_c)
    arrive(dot_copies)
    for k in range(1, n_clu):
        line = line + dots_c[k]
    spread_line = jnp.broadcast_to(line, (CLASSES, 128))
    bb, bq, qq, qt = [
        jnp.sum(
            jnp.where(lane == kind + k * CLASSES, spread_line, 0.0), axis=1, keepdims=True
        )
        for k in range(4)
    ]
    alpha = bb / (bb - bq)
    ratio = bq / bb
    norm = alpha * alpha * (qq - ratio * bq)
    beta = norm / bb
    h = beta - alpha * ratio
    curve = alpha * alpha * (qq - qt) + 2.0 * alpha * h * (bq - qq) + h * h * (bb - bq)
    alpha_next = norm / curve
    direction = alpha * first + h * labels
    image = alpha * (first - second) + h * (labels - first)
    scores_ref[...] = alpha * labels + alpha_next * direction
    residual_ref[...] = alpha * (first - ratio * labels) - alpha_next * image

    for copy in sent:
        copy.wait_send()


def on_device_dense(seed_class, seed_weight, tile_values, tile_rows, tile_cols, tile_count):
    n_clu = lax.axis_size("clu")
    n_mem = lax.axis_size("mem")
    _, _, slots, side, _ = tile_values.shape
    nodes = NB_DEV * side
    rows = nodes * n_mem
    cols = nodes * n_clu
    f32 = jnp.float32
    vmem = pl.BlockSpec(memory_space=pltpu.VMEM)
    hbm = pl.BlockSpec(memory_space=pltpu.HBM)
    w, row_total, col_total = pl.pallas_call(
        densify_kernel,
        out_shape=(
            jax.ShapeDtypeStruct((rows, cols), jnp.bfloat16),
            jax.ShapeDtypeStruct((n_mem, 1, nodes), f32),
            jax.ShapeDtypeStruct((n_clu, 1, nodes), f32),
        ),
        in_specs=[hbm, hbm, hbm, hbm],
        out_specs=(hbm, hbm, hbm),
        scratch_shapes=[
            pltpu.VMEM((rows, cols), jnp.bfloat16),
            pltpu.VMEM((n_mem, 1, nodes), f32),
            pltpu.VMEM((n_clu, 1, nodes), f32),
            pltpu.SMEM(tile_rows.shape, jnp.int32),
            pltpu.SMEM(tile_cols.shape, jnp.int32),
            pltpu.SMEM(tile_count.shape, jnp.int32),
            pltpu.VMEM((slots, side, side), tile_values.dtype),
            pltpu.VMEM((rows * cols // (side * side), side, side), f32),
            pltpu.SemaphoreType.DMA((3,)),
            pltpu.SemaphoreType.DMA((CHUNKS,)),
            pltpu.SemaphoreType.DMA((rows // side,)),
        ],
        compiler_params=pltpu.CompilerParams(vmem_limit_bytes=VMEM_LIMIT),
        name="densify",
    )(tile_rows, tile_cols, tile_count, tile_values)
    panel = (CLASSES, nodes)
    dma = pltpu.SemaphoreType.DMA
    return pl.pallas_call(
        functools.partial(solve_kernel, n_clu, n_mem),
        out_shape=(jax.ShapeDtypeStruct(panel, f32), jax.ShapeDtypeStruct(panel, f32)),
        in_specs=[hbm, hbm, hbm, hbm, hbm],
        out_specs=(vmem, vmem),
        scratch_shapes=[
            pltpu.VMEM((1, nodes), jnp.int32),
            pltpu.VMEM((1, nodes), f32),
            pltpu.VMEM((rows, cols), jnp.bfloat16),
            pltpu.VMEM((n_mem, 1, nodes), f32),
            pltpu.VMEM((n_clu, 1, nodes), f32),
            pltpu.VMEM((n_mem, 1, nodes), f32),
            pltpu.VMEM((n_clu, 1, nodes), f32),
            pltpu.VMEM((ITERS, *panel), f32),
            pltpu.VMEM((ITERS, n_mem, *panel), f32),
            pltpu.VMEM((ITERS, n_clu, *panel), f32),
            pltpu.VMEM((ITERS, n_mem, *panel), f32),
            pltpu.VMEM((ITERS, n_clu, *panel), f32),
            pltpu.VMEM((ITERS, n_mem, *panel), f32),
            pltpu.VMEM((ITERS, n_clu, *panel), f32),
            pltpu.VMEM((2, 1, 128), f32),
            pltpu.VMEM((n_mem, 1, 128), f32),
            pltpu.VMEM((n_clu, 1, 128), f32),
            dma((5,)),
            dma((2 + 2 * ITERS, n_mem)),
            dma((2 + 2 * ITERS, n_mem)),
            dma((2 + 2 * ITERS, n_clu)),
            dma((2 + 2 * ITERS, n_clu)),
        ],
        compiler_params=pltpu.CompilerParams(
            collective_id=0, has_side_effects=True, vmem_limit_bytes=VMEM_LIMIT
        ),
        name="solve",
    )(seed_class[None], seed_weight[None], w, row_total, col_total)


def on_device(seed_class, seed_weight, tile_values, tile_rows, tile_cols, tile_count):
    side = tile_values.shape[-1]
    blocks = NB_DEV * lax.axis_size("mem") * NB_DEV * lax.axis_size("clu")
    if blocks * side * side * 4 <= DENSE_LIMIT:
        run = on_device_dense
    else:
        run = on_device_slots
    return run(seed_class, seed_weight, tile_values, tile_rows, tile_cols, tile_count)


def solution(mesh):
    in_specs = (
        P(("clu", "mem")),
        P(("clu", "mem")),
        P("clu", "mem", None, None, None),
        P("clu", "mem", None),
        P("clu", "mem", None),
        P("clu", "mem"),
    )
    out_specs = (P(None, ("clu", "mem")), P(None, ("clu", "mem")))
    return jax.shard_map(
        on_device, mesh=mesh, in_specs=in_specs, out_specs=out_specs, check_vma=False
    )
```

```python
import functools
import jax
import jax.numpy as jnp
from jax import lax
from jax.experimental import pallas as pl
from jax.experimental.pallas import tpu as pltpu
from jax.sharding import PartitionSpec as P

CLASSES = 8
NB_DEV = 2
ITERS = 2
CHUNKS = 4
DENSE_LIMIT = 16 * 1024 * 1024
VMEM_LIMIT = 64 * 1024 * 1024
MESH = pl.DeviceIdType.MESH


def spread(row_part, col_part):
    width = row_part.shape[0]
    from_rows = lax.psum_scatter(
        row_part.reshape(width, -1), "mem", scatter_dimension=1, tiled=True
    )
    from_cols = lax.psum_scatter(
        col_part.reshape(width, -1), "clu", scatter_dimension=1, tiled=True
    )
    return from_rows + from_cols


def squares(residual):
    return lax.psum(jnp.sum(residual * residual, axis=1), ("clu", "mem"))


def on_device_slots(seed_class, seed_weight, tile_values, tile_rows, tile_cols, tile_count):
    tiles = tile_values[0, 0]
    rows = tile_rows[0, 0]
    cols = tile_cols[0, 0]
    count = tile_count[0, 0]
    slots = tiles.shape[0]
    side = tiles.shape[1]
    row_blocks = NB_DEV * lax.axis_size("mem")
    col_blocks = NB_DEV * lax.axis_size("clu")
    valid = (jnp.arange(slots, dtype=jnp.int32) < count).astype(jnp.float32)
    row_table = (rows[None, :] == jnp.arange(row_blocks, dtype=jnp.int32)[:, None]).astype(
        jnp.float32
    ) * valid[None, :]
    col_table = (cols[None, :] == jnp.arange(col_blocks, dtype=jnp.int32)[:, None]).astype(
        jnp.float32
    ) * valid[None, :]
    highest = lax.Precision.HIGHEST
    row_totals = jnp.sum(tiles, axis=2, dtype=jnp.float32)
    col_totals = jnp.sum(tiles, axis=1, dtype=jnp.float32)
    row_part = jnp.einsum("rt,ti->ri", row_table, row_totals, precision=highest)
    col_part = jnp.einsum("kt,tj->kj", col_table, col_totals, precision=highest)
    degree = 1.0 + spread(row_part[None], col_part[None])[0]
    inverse_root = lax.rsqrt(degree)
    classes_now = jnp.arange(CLASSES, dtype=jnp.int32)[:, None]
    labels = jnp.where(seed_class[None, :] == classes_now, seed_weight[None, :], jnp.float32(0.0))
    scores = jnp.zeros_like(labels)
    residual = labels
    direction = labels
    norm_now = squares(residual)
    for step in range(ITERS):
        width = direction.shape[0]
        scaled = (inverse_root[None, :] * direction).astype(jnp.bfloat16)
        col_panel = lax.all_gather(scaled, "clu", axis=1, tiled=True).reshape(
            width, col_blocks, side
        )
        row_panel = lax.all_gather(scaled, "mem", axis=1, tiled=True).reshape(
            width, row_blocks, side
        )
        forward = jnp.einsum(
            "tij,ctj->cti",
            tiles,
            jnp.take(col_panel, cols, axis=1),
            preferred_element_type=jnp.float32,
        )
        backward = jnp.einsum(
            "tij,cti->ctj",
            tiles,
            jnp.take(row_panel, rows, axis=1),
            preferred_element_type=jnp.float32,
        )
        row_sum = jnp.einsum("rt,cti->cri", row_table, forward, precision=highest)
        col_sum = jnp.einsum("kt,ctj->ckj", col_table, backward, precision=highest)
        image_sum = spread(row_sum, col_sum)
        image = direction - 0.99 * inverse_root[None, :] * image_sum
        alpha = norm_now / lax.psum(jnp.sum(direction * image, axis=1), ("clu", "mem"))
        scores = scores + alpha[:, None] * direction
        residual = residual - alpha[:, None] * image
        if step + 1 < ITERS:
            norm_next = squares(residual)
            direction = residual + (norm_next / norm_now)[:, None] * direction
            norm_now = norm_next
    return (scores, residual)


def densify_kernel(
    rows_hbm,
    cols_hbm,
    count_hbm,
    tiles_hbm,
    class_hbm,
    weight_hbm,
    w_hbm,
    sums_hbm,
    labels_hbm,
    w_ref,
    sums_ref,
    labels_ref,
    class_ref,
    weight_ref,
    rows_ref,
    cols_ref,
    count_ref,
    tiles,
    dense,
    small_sems,
    sems,
    out_sems,
):
    slots, side, _ = tiles.shape
    row_blocks = w_ref.shape[0] // side
    col_blocks = w_ref.shape[1] // side
    chunk = slots // CHUNKS
    small = [
        pltpu.make_async_copy(rows_hbm, rows_ref, small_sems.at[0]),
        pltpu.make_async_copy(cols_hbm, cols_ref, small_sems.at[1]),
        pltpu.make_async_copy(count_hbm, count_ref, small_sems.at[2]),
        pltpu.make_async_copy(class_hbm, class_ref, small_sems.at[3]),
        pltpu.make_async_copy(weight_hbm, weight_ref, small_sems.at[4]),
    ]
    for copy in small:
        copy.start()
    copies = [
        pltpu.make_async_copy(
            tiles_hbm.at[0, 0, pl.ds(k * chunk, chunk)], tiles.at[pl.ds(k * chunk, chunk)], sems.at[k]
        )
        for k in range(CHUNKS)
    ]
    for copy in copies:
        copy.start()

    def clear(k, carry):
        dense[k] = jnp.zeros((side, side), jnp.float32)
        return carry

    lax.fori_loop(0, row_blocks * col_blocks, clear, 0)
    for copy in small:
        copy.wait()
    count = count_ref[0, 0]
    kinds = lax.broadcasted_iota(jnp.int32, labels_ref.shape, 0)
    labels_ref[...] = jnp.where(class_ref[...] == kinds, weight_ref[...], jnp.float32(0.0))
    results = [
        pltpu.make_async_copy(labels_ref, labels_hbm, small_sems.at[0])
    ]
    results[0].start()

    def add(s, carry):
        place = rows_ref[0, 0, s] * col_blocks + cols_ref[0, 0, s]
        dense[place] += tiles[s].astype(jnp.float32)
        return carry

    for k in range(CHUNKS):
        copies[k].wait()
        lax.fori_loop(k * chunk, jnp.clip(count, k * chunk, (k + 1) * chunk), add, 0)

    members = row_blocks // NB_DEV
    col_sums = [jnp.zeros((8, side), jnp.float32) for _ in range(col_blocks)]
    for r in range(row_blocks):
        row_sum = jnp.zeros((side, side), jnp.float32)
        for c in range(col_blocks):
            block = dense[r * col_blocks + c]
            w_ref[r * side : (r + 1) * side, c * side : (c + 1) * side] = block.astype(jnp.bfloat16)
            row_sum = row_sum + block
            col_sums[c] = col_sums[c] + jnp.sum(block.reshape(side // 8, 8, side), axis=0)
        at = (r % NB_DEV) * side
        sums_ref[r // NB_DEV, :, at : at + side] = jnp.sum(row_sum.T, axis=0, keepdims=True)
        strip = pl.ds(r * side, side)
        results.append(pltpu.make_async_copy(w_ref.at[strip], w_hbm.at[strip], out_sems.at[r]))
        results[-1].start()
    for c in range(col_blocks):
        at = (c % NB_DEV) * side
        sums_ref[members + c // NB_DEV, :, at : at + side] = jnp.sum(col_sums[c], axis=0, keepdims=True)
    results.append(pltpu.make_async_copy(sums_ref, sums_hbm, small_sems.at[1]))
    results[-1].start()
    for copy in results:
        copy.wait()


def split(panel):
    high = panel.astype(jnp.bfloat16)
    low = (panel - high.astype(jnp.float32)).astype(jnp.bfloat16)
    return jnp.concatenate([high, low], axis=0)


def solve_kernel(
    n_clu,
    n_mem,
    w_hbm,
    sums_hbm,
    labels_hbm,
    scores_ref,
    residual_ref,
    w,
    sums_ref,
    labels_ref,
    deg_m,
    deg_c,
    own,
    pan_m,
    pan_c,
    part_m,
    part_c,
    got_m,
    got_c,
    dots,
    dots_m,
    dots_c,
    load_sems,
    send_m,
    recv_m,
    send_c,
    recv_c,
):
    me_c = lax.axis_index("clu")
    me_m = lax.axis_index("mem")
    others_m = [None] + [lax.rem(me_m + k, n_mem) for k in range(1, n_mem)]
    others_c = [None] + [lax.rem(me_c + k, n_clu) for k in range(1, n_clu)]

    loads = [
        pltpu.make_async_copy(sums_hbm, sums_ref, load_sems.at[0]),
        pltpu.make_async_copy(labels_hbm, labels_ref, load_sems.at[1]),
    ]
    w_copy = pltpu.make_async_copy(w_hbm, w, load_sems.at[2])
    for copy in loads:
        copy.start()
    w_copy.start()
    barrier = pltpu.get_barrier_semaphore()
    for k in range(1, n_mem):
        pl.semaphore_signal(barrier, device_id=(me_c, others_m[k]), device_id_type=MESH)
    for k in range(1, n_clu):
        pl.semaphore_signal(barrier, device_id=(others_c[k], me_m), device_id_type=MESH)

    sent = []

    def whole(room, count, send_sem, recv_sem):
        view = room.at[pl.ds(0, count - 1)]
        sent.append(pltpu.make_async_copy(view, view, send_sem))
        return pltpu.make_async_copy(view, view, recv_sem)

    def over_mem(phase, source, target, room):
        for k in range(1, n_mem):
            pltpu.make_async_remote_copy(
                src_ref=source(others_m[k]),
                dst_ref=target(k),
                send_sem=send_m.at[phase],
                recv_sem=recv_m.at[phase],
                device_id=(me_c, others_m[k]),
                device_id_type=MESH,
            ).start()
        return whole(room, n_mem, send_m.at[phase], recv_m.at[phase])

    def over_clu(phase, source, target, room):
        for k in range(1, n_clu):
            pltpu.make_async_remote_copy(
                src_ref=source(others_c[k]),
                dst_ref=target(k),
                send_sem=send_c.at[phase],
                recv_sem=recv_c.at[phase],
                device_id=(others_c[k], me_m),
                device_id_type=MESH,
            ).start()
        return whole(room, n_clu, send_c.at[phase], recv_c.at[phase])

    for copy in loads:
        copy.wait()
    labels = labels_ref[...]
    pl.semaphore_wait(barrier, n_mem + n_clu - 2)

    from_m = over_mem(0, lambda o: sums_ref.at[o], lambda k: deg_m.at[k], deg_m)
    from_c = over_clu(0, lambda o: sums_ref.at[n_mem + o], lambda k: deg_c.at[k], deg_c)
    degree = 1.0 + (sums_ref[me_m] + sums_ref[n_mem + me_c])
    from_m.wait()
    for k in range(1, n_mem):
        degree = degree + deg_m[k]
    from_c.wait()
    for k in range(1, n_clu):
        degree = degree + deg_c[k]
    root = lax.rsqrt(degree)

    def gather(step, panel):
        own[step] = panel
        pan_m[step, me_m] = panel
        pan_c[step, me_c] = panel
        from_m = over_mem(1 + 2 * step, lambda o: own.at[step], lambda k: pan_m.at[step, me_m], pan_m.at[step])
        from_c = over_clu(1 + 2 * step, lambda o: own.at[step], lambda k: pan_c.at[step, me_c], pan_c.at[step])
        return from_m, from_c

    def multiply(step, from_m, from_c, prepare, between):
        phase = 2 + 2 * step
        from_m.wait()
        left = jnp.concatenate([pan_m[step, k] for k in range(n_mem)], axis=1)
        if step == 0:
            w_copy.wait()
        out = lax.dot_general(
            prepare(left), w[...], (((1,), (0,)), ((), ())), preferred_element_type=jnp.float32
        )
        out = out[:CLASSES] if step == 0 else out[:CLASSES] + out[CLASSES:]
        width = out.shape[1] // n_clu
        for k in range(n_clu):
            part_c[step, k] = out[:, k * width : (k + 1) * width]
        back_c = over_clu(phase, lambda o: part_c.at[step, o], lambda k: got_c.at[step, k], got_c.at[step])
        from_c.wait()
        right = jnp.concatenate([pan_c[step, k] for k in range(n_clu)], axis=1)
        between(right, out)
        out = lax.dot_general(
            prepare(right), w[...], (((1,), (1,)), ((), ())), preferred_element_type=jnp.float32
        )
        out = out[:CLASSES] if step == 0 else out[:CLASSES] + out[CLASSES:]
        for k in range(n_mem):
            part_m[step, k] = out[:, k * width : (k + 1) * width]
        back_m = over_mem(phase, lambda o: part_m.at[step, o], lambda k: got_m.at[step, k], got_m.at[step])
        return back_m, back_c

    def collect(step, back_m, back_c):
        image = part_m[step, me_m] + part_c[step, me_c]
        back_c.wait()
        for k in range(1, n_clu):
            image = image + got_c[step, k]
        back_m.wait()
        for k in range(1, n_mem):
            image = image + got_m[step, k]
        return 0.99 * root * image

    from_m, from_c = gather(0, root * labels)
    back_m, back_c = multiply(
        0, from_m, from_c, lambda x: x.astype(jnp.bfloat16), lambda right, out: None
    )
    first = collect(0, back_m, back_c)

    from_m, from_c = gather(1, root * first)
    lane = lax.broadcasted_iota(jnp.int32, (CLASSES, 128), 1)
    kind = lax.broadcasted_iota(jnp.int32, (CLASSES, 128), 0)
    sums = [
        jnp.sum(labels * labels, axis=1, keepdims=True),
        jnp.sum(labels * first, axis=1, keepdims=True),
        jnp.sum(first * first, axis=1, keepdims=True),
    ]
    dot_copies = []

    def send_sums(right, image):
        cross = 1.98 * jnp.sum(right * image, axis=1, keepdims=True)
        line = jnp.zeros((CLASSES, 128), jnp.float32)
        for k, value in enumerate([*sums, cross]):
            line = line + jnp.where(lane == kind + k * CLASSES, value, 0.0)
        dots[0] = jnp.sum(line, axis=0, keepdims=True)
        dot_copies.append(over_mem(5, lambda o: dots.at[0], lambda k: dots_m.at[k], dots_m))

    back_m, back_c = multiply(1, from_m, from_c, split, send_sums)
    dot_copies[0].wait()
    line = dots[0]
    for k in range(1, n_mem):
        line = line + dots_m[k]
    dots[1] = line
    dot_copies.append(over_clu(5, lambda o: dots.at[1], lambda k: dots_c.at[k], dots_c))
    second = collect(1, back_m, back_c)
    dot_copies[1].wait()
    for k in range(1, n_clu):
        line = line + dots_c[k]
    spread_line = jnp.broadcast_to(line, (CLASSES, 128))
    bb, bq, qq, qt = [
        jnp.sum(
            jnp.where(lane == kind + k * CLASSES, spread_line, 0.0), axis=1, keepdims=True
        )
        for k in range(4)
    ]
    alpha = bb / (bb - bq)
    ratio = bq / bb
    norm = alpha * alpha * (qq - ratio * bq)
    beta = norm / bb
    h = beta - alpha * ratio
    curve = alpha * alpha * (qq - qt) + 2.0 * alpha * h * (bq - qq) + h * h * (bb - bq)
    alpha_next = norm / curve
    direction = alpha * first + h * labels
    image = alpha * (first - second) + h * (labels - first)
    scores_ref[...] = alpha * labels + alpha_next * direction
    residual_ref[...] = alpha * (first - ratio * labels) - alpha_next * image

    for copy in sent:
        copy.wait()


def finish_kernel(scores_in, residual_in, scores_out, residual_out, sems):
    copies = [
        pltpu.make_async_copy(scores_in, scores_out, sems.at[0]),
        pltpu.make_async_copy(residual_in, residual_out, sems.at[1]),
    ]
    for copy in copies:
        copy.start()
    for copy in copies:
        copy.wait()


def on_device_dense(seed_class, seed_weight, tile_values, tile_rows, tile_cols, tile_count):
    n_clu = lax.axis_size("clu")
    n_mem = lax.axis_size("mem")
    _, _, slots, side, _ = tile_values.shape
    nodes = NB_DEV * side
    rows = nodes * n_mem
    cols = nodes * n_clu
    f32 = jnp.float32
    vmem = pl.BlockSpec(memory_space=pltpu.VMEM)
    hbm = pl.BlockSpec(memory_space=pltpu.HBM)
    panel = (CLASSES, nodes)
    w, sums, labels = pl.pallas_call(
        densify_kernel,
        out_shape=(
            jax.ShapeDtypeStruct((rows, cols), jnp.bfloat16),
            jax.ShapeDtypeStruct((n_mem + n_clu, 1, nodes), f32),
            jax.ShapeDtypeStruct(panel, f32),
        ),
        in_specs=[hbm] * 6,
        out_specs=(hbm, hbm, hbm),
        scratch_shapes=[
            pltpu.VMEM((rows, cols), jnp.bfloat16),
            pltpu.VMEM((n_mem + n_clu, 1, nodes), f32),
            pltpu.VMEM(panel, f32),
            pltpu.VMEM((1, nodes), jnp.int32),
            pltpu.VMEM((1, nodes), f32),
            pltpu.SMEM(tile_rows.shape, jnp.int32),
            pltpu.SMEM(tile_cols.shape, jnp.int32),
            pltpu.SMEM(tile_count.shape, jnp.int32),
            pltpu.VMEM((slots, side, side), tile_values.dtype),
            pltpu.VMEM((rows * cols // (side * side), side, side), f32),
            pltpu.SemaphoreType.DMA((5,)),
            pltpu.SemaphoreType.DMA((CHUNKS,)),
            pltpu.SemaphoreType.DMA((rows // side,)),
        ],
        compiler_params=pltpu.CompilerParams(vmem_limit_bytes=VMEM_LIMIT),
        name="densify",
    )(tile_rows, tile_cols, tile_count, tile_values, seed_class[None], seed_weight[None])
    dma = pltpu.SemaphoreType.DMA
    results = (jax.ShapeDtypeStruct(panel, f32), jax.ShapeDtypeStruct(panel, f32))
    found = pl.pallas_call(
        functools.partial(solve_kernel, n_clu, n_mem),
        out_shape=results,
        in_specs=[hbm] * 3,
        out_specs=(vmem, vmem),
        scratch_shapes=[
            pltpu.VMEM((rows, cols), jnp.bfloat16),
            pltpu.VMEM((n_mem + n_clu, 1, nodes), f32),
            pltpu.VMEM(panel, f32),
            pltpu.VMEM((n_mem, 1, nodes), f32),
            pltpu.VMEM((n_clu, 1, nodes), f32),
            pltpu.VMEM((ITERS, *panel), f32),
            pltpu.VMEM((ITERS, n_mem, *panel), f32),
            pltpu.VMEM((ITERS, n_clu, *panel), f32),
            pltpu.VMEM((ITERS, n_mem, *panel), f32),
            pltpu.VMEM((ITERS, n_clu, *panel), f32),
            pltpu.VMEM((ITERS, n_mem, *panel), f32),
            pltpu.VMEM((ITERS, n_clu, *panel), f32),
            pltpu.VMEM((2, 1, 128), f32),
            pltpu.VMEM((n_mem, 1, 128), f32),
            pltpu.VMEM((n_clu, 1, 128), f32),
            dma((3,)),
            dma((2 + 2 * ITERS,)),
            dma((2 + 2 * ITERS,)),
            dma((2 + 2 * ITERS,)),
            dma((2 + 2 * ITERS,)),
        ],
        compiler_params=pltpu.CompilerParams(
            collective_id=0, has_side_effects=True, vmem_limit_bytes=VMEM_LIMIT
        ),
        name="solve",
    )(w, sums, labels)
    return pl.pallas_call(
        finish_kernel,
        out_shape=results,
        in_specs=[hbm, hbm],
        out_specs=(hbm, hbm),
        scratch_shapes=[dma((2,))],
        compiler_params=pltpu.CompilerParams(vmem_limit_bytes=VMEM_LIMIT),
        name="finish",
    )(*found)


def on_device(seed_class, seed_weight, tile_values, tile_rows, tile_cols, tile_count):
    side = tile_values.shape[-1]
    blocks = NB_DEV * lax.axis_size("mem") * NB_DEV * lax.axis_size("clu")
    if blocks * side * side * 4 <= DENSE_LIMIT:
        run = on_device_dense
    else:
        run = on_device_slots
    return run(seed_class, seed_weight, tile_values, tile_rows, tile_cols, tile_count)


def solution(mesh):
    in_specs = (
        P(("clu", "mem")),
        P(("clu", "mem")),
        P("clu", "mem", None, None, None),
        P("clu", "mem", None),
        P("clu", "mem", None),
        P("clu", "mem"),
    )
    out_specs = (P(None, ("clu", "mem")), P(None, ("clu", "mem")))
    return jax.shard_map(
        on_device, mesh=mesh, in_specs=in_specs, out_specs=out_specs, check_vma=False
    )
```

```python
import functools
import jax
import jax.numpy as jnp
from jax import lax
from jax.experimental import pallas as pl
from jax.experimental.pallas import tpu as pltpu
from jax.sharding import PartitionSpec as P

CLASSES = 8
NB_DEV = 2
ITERS = 2
GROUP = 16
PACK = 4
TABLE_LIMIT = 16 * 1024 * 1024
VMEM_LIMIT = 64 * 1024 * 1024
MESH = pl.DeviceIdType.MESH


def spread(row_part, col_part):
    width = row_part.shape[0]
    from_rows = lax.psum_scatter(
        row_part.reshape(width, -1), "mem", scatter_dimension=1, tiled=True
    )
    from_cols = lax.psum_scatter(
        col_part.reshape(width, -1), "clu", scatter_dimension=1, tiled=True
    )
    return from_rows + from_cols


def squares(residual):
    return lax.psum(jnp.sum(residual * residual, axis=1), ("clu", "mem"))


def on_device_slots(seed_class, seed_weight, tile_values, tile_rows, tile_cols, tile_count):
    tiles = tile_values[0, 0]
    rows = tile_rows[0, 0]
    cols = tile_cols[0, 0]
    count = tile_count[0, 0]
    slots = tiles.shape[0]
    side = tiles.shape[1]
    row_blocks = NB_DEV * lax.axis_size("mem")
    col_blocks = NB_DEV * lax.axis_size("clu")
    valid = (jnp.arange(slots, dtype=jnp.int32) < count).astype(jnp.float32)
    row_table = (rows[None, :] == jnp.arange(row_blocks, dtype=jnp.int32)[:, None]).astype(
        jnp.float32
    ) * valid[None, :]
    col_table = (cols[None, :] == jnp.arange(col_blocks, dtype=jnp.int32)[:, None]).astype(
        jnp.float32
    ) * valid[None, :]
    highest = lax.Precision.HIGHEST
    row_totals = jnp.sum(tiles, axis=2, dtype=jnp.float32)
    col_totals = jnp.sum(tiles, axis=1, dtype=jnp.float32)
    row_part = jnp.einsum("rt,ti->ri", row_table, row_totals, precision=highest)
    col_part = jnp.einsum("kt,tj->kj", col_table, col_totals, precision=highest)
    degree = 1.0 + spread(row_part[None], col_part[None])[0]
    inverse_root = lax.rsqrt(degree)
    classes_now = jnp.arange(CLASSES, dtype=jnp.int32)[:, None]
    labels = jnp.where(seed_class[None, :] == classes_now, seed_weight[None, :], jnp.float32(0.0))
    scores = jnp.zeros_like(labels)
    residual = labels
    direction = labels
    norm_now = squares(residual)
    for step in range(ITERS):
        width = direction.shape[0]
        scaled = (inverse_root[None, :] * direction).astype(jnp.bfloat16)
        col_panel = lax.all_gather(scaled, "clu", axis=1, tiled=True).reshape(
            width, col_blocks, side
        )
        row_panel = lax.all_gather(scaled, "mem", axis=1, tiled=True).reshape(
            width, row_blocks, side
        )
        forward = jnp.einsum(
            "tij,ctj->cti",
            tiles,
            jnp.take(col_panel, cols, axis=1),
            preferred_element_type=jnp.float32,
        )
        backward = jnp.einsum(
            "tij,cti->ctj",
            tiles,
            jnp.take(row_panel, rows, axis=1),
            preferred_element_type=jnp.float32,
        )
        row_sum = jnp.einsum("rt,cti->cri", row_table, forward, precision=highest)
        col_sum = jnp.einsum("kt,ctj->ckj", col_table, backward, precision=highest)
        image_sum = spread(row_sum, col_sum)
        image = direction - 0.99 * inverse_root[None, :] * image_sum
        alpha = norm_now / lax.psum(jnp.sum(direction * image, axis=1), ("clu", "mem"))
        scores = scores + alpha[:, None] * direction
        residual = residual - alpha[:, None] * image
        if step + 1 < ITERS:
            norm_next = squares(residual)
            direction = residual + (norm_next / norm_now)[:, None] * direction
            norm_now = norm_next
    return (scores, residual)


def solve_kernel(
    n_clu,
    n_mem,
    class_hbm,
    weight_hbm,
    tiles_hbm,
    rows_hbm,
    cols_hbm,
    count_hbm,
    scores_ref,
    residual_ref,
    class_ref,
    weight_ref,
    rows_ref,
    cols_ref,
    count_ref,
    tiles,
    hot_rows,
    hot_cols,
    from_rows,
    from_cols,
    sums_ref,
    deg_m,
    deg_c,
    own,
    pan_m,
    pan_c,
    part_m,
    part_c,
    got_m,
    got_c,
    dots,
    dots_m,
    dots_c,
    load_sems,
    tile_sems,
    send_m,
    recv_m,
    send_c,
    recv_c,
):
    me_c = lax.axis_index("clu")
    me_m = lax.axis_index("mem")
    others_m = [None] + [lax.rem(me_m + k, n_mem) for k in range(1, n_mem)]
    others_c = [None] + [lax.rem(me_c + k, n_clu) for k in range(1, n_clu)]

    slots, side, _ = tiles.shape
    row_blocks = NB_DEV * n_mem
    col_blocks = NB_DEV * n_clu
    steps = slots // GROUP

    loads = [
        pltpu.make_async_copy(rows_hbm, rows_ref, load_sems.at[0]),
        pltpu.make_async_copy(cols_hbm, cols_ref, load_sems.at[1]),
        pltpu.make_async_copy(count_hbm, count_ref, load_sems.at[2]),
        pltpu.make_async_copy(class_hbm, class_ref, load_sems.at[3]),
        pltpu.make_async_copy(weight_hbm, weight_ref, load_sems.at[4]),
    ]

    def tile_copy(g):
        part = pl.ds(g * GROUP, GROUP)
        return pltpu.make_async_copy(tiles_hbm.at[0, 0, part], tiles.at[part], tile_sems.at[g])

    for copy in loads:
        copy.start()
    for g in range(steps):
        tile_copy(g).start()
    barrier = pltpu.get_barrier_semaphore()
    for k in range(1, n_mem):
        pl.semaphore_signal(barrier, device_id=(me_c, others_m[k]), device_id_type=MESH)
    for k in range(1, n_clu):
        pl.semaphore_signal(barrier, device_id=(others_c[k], me_m), device_id_type=MESH)

    sent = []

    def whole(room, count, send_sem, recv_sem):
        view = room.at[pl.ds(0, count - 1)]
        sent.append(pltpu.make_async_copy(view, view, send_sem))
        return pltpu.make_async_copy(view, view, recv_sem)

    def over_mem(phase, source, target, room):
        for k in range(1, n_mem):
            pltpu.make_async_remote_copy(
                src_ref=source(others_m[k]),
                dst_ref=target(k),
                send_sem=send_m.at[phase],
                recv_sem=recv_m.at[phase],
                device_id=(me_c, others_m[k]),
                device_id_type=MESH,
            ).start()
        return whole(room, n_mem, send_m.at[phase], recv_m.at[phase])

    def over_clu(phase, source, target, room):
        for k in range(1, n_clu):
            pltpu.make_async_remote_copy(
                src_ref=source(others_c[k]),
                dst_ref=target(k),
                send_sem=send_c.at[phase],
                recv_sem=recv_c.at[phase],
                device_id=(others_c[k], me_m),
                device_id_type=MESH,
            ).start()
        return whole(room, n_clu, send_c.at[phase], recv_c.at[phase])

    for copy in loads:
        copy.wait()
    count = count_ref[0, 0]
    kinds = lax.broadcasted_iota(jnp.int32, (CLASSES, weight_ref.shape[1]), 0)
    labels = jnp.where(class_ref[...] == kinds, weight_ref[...], jnp.float32(0.0))

    for blocks, hot in ((row_blocks, hot_rows), (col_blocks, hot_cols)):
        at = lax.broadcasted_iota(jnp.int32, (blocks, side), 0)
        for k in range(blocks + 1):
            hot[k] = jnp.where(at == k, jnp.float32(1.0), jnp.float32(0.0))
    from_rows[...] = jnp.zeros_like(from_rows)
    from_cols[...] = jnp.zeros_like(from_cols)

    def used(slot, block, blocks):
        unused = 1 - jnp.clip(count - slot, 0, 1)
        return block + (blocks - block) * unused

    def dot_rows(left, slot):
        return lax.dot_general(
            left, tiles[slot], (((1,), (1,)), ((), ())), preferred_element_type=jnp.float32
        )

    def dot_cols(left, slot):
        right = tiles[pl.ds(slot, PACK)].reshape(PACK * side, side)
        return lax.dot_general(
            left, right, (((1,), (0,)), ((), ())), preferred_element_type=jnp.float32
        )

    def add_totals(g, carry):
        row_total, col_total = carry
        tile_copy(g).wait()
        for k in range(0, GROUP, PACK):
            packed = []
            for slot in [g * GROUP + k + e for e in range(PACK)]:
                row = used(slot, rows_ref[0, 0, slot], row_blocks)
                col = used(slot, cols_ref[0, 0, slot], col_blocks)
                row_total = row_total + dot_rows(hot_rows[row].astype(jnp.bfloat16), slot)
                packed.append(hot_cols[col].astype(jnp.bfloat16))
            col_total = col_total + dot_cols(jnp.concatenate(packed, axis=1), g * GROUP + k)
        return row_total, col_total

    row_total, col_total = lax.fori_loop(
        0,
        steps,
        add_totals,
        (jnp.zeros((row_blocks, side), jnp.float32), jnp.zeros((col_blocks, side), jnp.float32)),
    )
    for k in range(row_blocks):
        at = k % NB_DEV * side
        sums_ref[k // NB_DEV, :, at : at + side] = row_total[k : k + 1]
    for k in range(col_blocks):
        at = k % NB_DEV * side
        sums_ref[n_mem + k // NB_DEV, :, at : at + side] = col_total[k : k + 1]

    def column_sums():
        def step(g, total):
            for k in range(0, GROUP, PACK):
                packed = []
                for slot in [g * GROUP + k + e for e in range(PACK)]:
                    row = used(slot, rows_ref[0, 0, slot], row_blocks)
                    start = col_blocks - 1 - cols_ref[0, 0, slot]
                    left = from_rows[row, pl.ds(start, col_blocks)]
                    packed.append(left.reshape(col_blocks * CLASSES, side).astype(jnp.bfloat16))
                total = total + dot_cols(jnp.concatenate(packed, axis=1), g * GROUP + k)
            return total

        zero = jnp.zeros((col_blocks * CLASSES, side), jnp.float32)
        return lax.fori_loop(0, steps, step, zero)

    def row_sums():
        def step(g, total):
            for slot in [g * GROUP + k for k in range(GROUP)]:
                col = used(slot, cols_ref[0, 0, slot], col_blocks)
                start = row_blocks - 1 - rows_ref[0, 0, slot]
                left = from_cols[col, pl.ds(start, row_blocks)]
                left = left.reshape(row_blocks * CLASSES, side).astype(jnp.bfloat16)
                total = total + dot_rows(left, slot)
            return total

        zero = jnp.zeros((row_blocks * CLASSES, side), jnp.float32)
        return lax.fori_loop(0, steps, step, zero)

    pl.semaphore_wait(barrier, n_mem + n_clu - 2)

    from_m = over_mem(0, lambda o: sums_ref.at[o], lambda k: deg_m.at[k], deg_m)
    from_c = over_clu(0, lambda o: sums_ref.at[n_mem + o], lambda k: deg_c.at[k], deg_c)
    degree = 1.0 + (sums_ref[me_m] + sums_ref[n_mem + me_c])
    from_m.wait()
    for k in range(1, n_mem):
        degree = degree + deg_m[k]
    from_c.wait()
    for k in range(1, n_clu):
        degree = degree + deg_c[k]
    root = lax.rsqrt(degree)

    def gather(step, panel):
        own[step] = panel
        pan_m[step, me_m] = panel
        pan_c[step, me_c] = panel
        from_m = over_mem(1 + 2 * step, lambda o: own.at[step], lambda k: pan_m.at[step, me_m], pan_m.at[step])
        from_c = over_clu(1 + 2 * step, lambda o: own.at[step], lambda k: pan_c.at[step, me_c], pan_c.at[step])
        return from_m, from_c

    def blocks_of(panels):
        for owner, panel in enumerate(panels):
            for k in range(NB_DEV):
                yield owner * NB_DEV + k, panel[:, k * side : (k + 1) * side]

    def multiply(step, from_m, from_c, between):
        phase = 2 + 2 * step
        from_m.wait()
        for k, block in blocks_of([pan_m[step, k] for k in range(n_mem)]):
            from_rows[k, col_blocks - 1] = block
        out = column_sums()
        for k in range(col_blocks):
            at = k % NB_DEV * side
            part_c[step, k // NB_DEV, :, at : at + side] = out[k * CLASSES : (k + 1) * CLASSES]
        back_c = over_clu(
            phase, lambda o: part_c.at[step, o], lambda k: got_c.at[step, k], got_c.at[step]
        )
        from_c.wait()
        panels = [pan_c[step, k] for k in range(n_clu)]
        for k, block in blocks_of(panels):
            from_cols[k, row_blocks - 1] = block
        between(panels)
        out = row_sums()
        for k in range(row_blocks):
            at = k % NB_DEV * side
            part_m[step, k // NB_DEV, :, at : at + side] = out[k * CLASSES : (k + 1) * CLASSES]
        back_m = over_mem(
            phase, lambda o: part_m.at[step, o], lambda k: got_m.at[step, k], got_m.at[step]
        )
        return back_m, back_c

    def collect(step, back_m, back_c):
        image = part_m[step, me_m] + part_c[step, me_c]
        back_c.wait()
        for k in range(1, n_clu):
            image = image + got_c[step, k]
        back_m.wait()
        for k in range(1, n_mem):
            image = image + got_m[step, k]
        return 0.99 * root * image

    from_m, from_c = gather(0, root * labels)
    back_m, back_c = multiply(0, from_m, from_c, lambda panels: None)
    first = collect(0, back_m, back_c)

    from_m, from_c = gather(1, root * first)
    lane = lax.broadcasted_iota(jnp.int32, (CLASSES, 128), 1)
    kind = lax.broadcasted_iota(jnp.int32, (CLASSES, 128), 0)
    sums = [
        jnp.sum(labels * labels, axis=1, keepdims=True),
        jnp.sum(labels * first, axis=1, keepdims=True),
        jnp.sum(first * first, axis=1, keepdims=True),
    ]
    dot_copies = []

    def send_sums(panels):
        cross = panels[0] * part_c[1, 0]
        for k in range(1, n_clu):
            cross = cross + panels[k] * part_c[1, k]
        cross = 1.98 * jnp.sum(cross, axis=1, keepdims=True)
        line = jnp.zeros((CLASSES, 128), jnp.float32)
        for k, value in enumerate([*sums, cross]):
            line = line + jnp.where(lane == kind + k * CLASSES, value, 0.0)
        dots[0] = jnp.sum(line, axis=0, keepdims=True)
        dot_copies.append(over_mem(5, lambda o: dots.at[0], lambda k: dots_m.at[k], dots_m))

    back_m, back_c = multiply(1, from_m, from_c, send_sums)
    dot_copies[0].wait()
    line = dots[0]
    for k in range(1, n_mem):
        line = line + dots_m[k]
    dots[1] = line
    dot_copies.append(over_clu(5, lambda o: dots.at[1], lambda k: dots_c.at[k], dots_c))
    second = collect(1, back_m, back_c)
    dot_copies[1].wait()
    for k in range(1, n_clu):
        line = line + dots_c[k]
    spread_line = jnp.broadcast_to(line, (CLASSES, 128))
    bb, bq, qq, qt = [
        jnp.sum(
            jnp.where(lane == kind + k * CLASSES, spread_line, 0.0), axis=1, keepdims=True
        )
        for k in range(4)
    ]
    alpha = bb / (bb - bq)
    ratio = bq / bb
    norm = alpha * alpha * (qq - ratio * bq)
    beta = norm / bb
    h = beta - alpha * ratio
    curve = alpha * alpha * (qq - qt) + 2.0 * alpha * h * (bq - qq) + h * h * (bb - bq)
    alpha_next = norm / curve
    direction = alpha * first + h * labels
    image = alpha * (first - second) + h * (labels - first)
    scores_ref[...] = alpha * labels + alpha_next * direction
    residual_ref[...] = alpha * (first - ratio * labels) - alpha_next * image

    for copy in sent:
        copy.wait()


def finish_kernel(scores_in, residual_in, scores_out, residual_out, sems):
    copies = [
        pltpu.make_async_copy(scores_in, scores_out, sems.at[0]),
        pltpu.make_async_copy(residual_in, residual_out, sems.at[1]),
    ]
    for copy in copies:
        copy.start()
    for copy in copies:
        copy.wait()


def on_device_kernel(seed_class, seed_weight, tile_values, tile_rows, tile_cols, tile_count):
    n_clu = lax.axis_size("clu")
    n_mem = lax.axis_size("mem")
    _, _, slots, side, _ = tile_values.shape
    nodes = NB_DEV * side
    row_blocks = NB_DEV * n_mem
    col_blocks = NB_DEV * n_clu
    f32 = jnp.float32
    hbm = pl.BlockSpec(memory_space=pltpu.HBM)
    vmem = pl.BlockSpec(memory_space=pltpu.VMEM)
    dma = pltpu.SemaphoreType.DMA
    panel = (CLASSES, nodes)
    results = (jax.ShapeDtypeStruct(panel, f32), jax.ShapeDtypeStruct(panel, f32))
    found = pl.pallas_call(
        functools.partial(solve_kernel, n_clu, n_mem),
        out_shape=results,
        in_specs=[hbm] * 6,
        out_specs=(vmem, vmem),
        scratch_shapes=[
            pltpu.VMEM((1, nodes), jnp.int32),
            pltpu.VMEM((1, nodes), f32),
            pltpu.SMEM(tile_rows.shape, jnp.int32),
            pltpu.SMEM(tile_cols.shape, jnp.int32),
            pltpu.SMEM(tile_count.shape, jnp.int32),
            pltpu.VMEM((slots, side, side), tile_values.dtype),
            pltpu.VMEM((row_blocks + 1, row_blocks, side), f32),
            pltpu.VMEM((col_blocks + 1, col_blocks, side), f32),
            pltpu.VMEM((row_blocks + 1, 2 * col_blocks - 1, CLASSES, side), f32),
            pltpu.VMEM((col_blocks + 1, 2 * row_blocks - 1, CLASSES, side), f32),
            pltpu.VMEM((n_mem + n_clu, 1, nodes), f32),
            pltpu.VMEM((n_mem, 1, nodes), f32),
            pltpu.VMEM((n_clu, 1, nodes), f32),
            pltpu.VMEM((ITERS, *panel), f32),
            pltpu.VMEM((ITERS, n_mem, *panel), f32),
            pltpu.VMEM((ITERS, n_clu, *panel), f32),
            pltpu.VMEM((ITERS, n_mem, *panel), f32),
            pltpu.VMEM((ITERS, n_clu, *panel), f32),
            pltpu.VMEM((ITERS, n_mem, *panel), f32),
            pltpu.VMEM((ITERS, n_clu, *panel), f32),
            pltpu.VMEM((2, 1, 128), f32),
            pltpu.VMEM((n_mem, 1, 128), f32),
            pltpu.VMEM((n_clu, 1, 128), f32),
            dma((5,)),
            dma((slots // GROUP,)),
            dma((2 + 2 * ITERS,)),
            dma((2 + 2 * ITERS,)),
            dma((2 + 2 * ITERS,)),
            dma((2 + 2 * ITERS,)),
        ],
        compiler_params=pltpu.CompilerParams(
            collective_id=0, has_side_effects=True, vmem_limit_bytes=VMEM_LIMIT
        ),
        name="solve",
    )(seed_class[None], seed_weight[None], tile_values, tile_rows, tile_cols, tile_count)
    return pl.pallas_call(
        finish_kernel,
        out_shape=results,
        in_specs=[hbm, hbm],
        out_specs=(hbm, hbm),
        scratch_shapes=[dma((2,))],
        compiler_params=pltpu.CompilerParams(vmem_limit_bytes=VMEM_LIMIT),
        name="finish",
    )(*found)


def on_device(seed_class, seed_weight, tile_values, tile_rows, tile_cols, tile_count):
    side = tile_values.shape[-1]
    blocks = NB_DEV * lax.axis_size("mem") * NB_DEV * lax.axis_size("clu")
    if blocks * CLASSES * side * 16 <= TABLE_LIMIT:
        run = on_device_kernel
    else:
        run = on_device_slots
    return run(seed_class, seed_weight, tile_values, tile_rows, tile_cols, tile_count)


def solution(mesh):
    in_specs = (
        P(("clu", "mem")),
        P(("clu", "mem")),
        P("clu", "mem", None, None, None),
        P("clu", "mem", None),
        P("clu", "mem", None),
        P("clu", "mem"),
    )
    out_specs = (P(None, ("clu", "mem")), P(None, ("clu", "mem")))
    return jax.shard_map(
        on_device, mesh=mesh, in_specs=in_specs, out_specs=out_specs, check_vma=False
    )
```

```python
import functools
import jax
import jax.numpy as jnp
from jax import lax
from jax.experimental import pallas as pl
from jax.experimental.pallas import tpu as pltpu
from jax.sharding import PartitionSpec as P

CLASSES = 8
NB_DEV = 2
ITERS = 2
GROUP = 16
SPAN = 48
PACK = 4
TABLE_LIMIT = 16 * 1024 * 1024
VMEM_LIMIT = 64 * 1024 * 1024
MESH = pl.DeviceIdType.MESH


def spread(row_part, col_part):
    width = row_part.shape[0]
    from_rows = lax.psum_scatter(
        row_part.reshape(width, -1), "mem", scatter_dimension=1, tiled=True
    )
    from_cols = lax.psum_scatter(
        col_part.reshape(width, -1), "clu", scatter_dimension=1, tiled=True
    )
    return from_rows + from_cols


def squares(residual):
    return lax.psum(jnp.sum(residual * residual, axis=1), ("clu", "mem"))


def on_device_slots(seed_class, seed_weight, tile_values, tile_rows, tile_cols, tile_count):
    tiles = tile_values[0, 0]
    rows = tile_rows[0, 0]
    cols = tile_cols[0, 0]
    count = tile_count[0, 0]
    slots = tiles.shape[0]
    side = tiles.shape[1]
    row_blocks = NB_DEV * lax.axis_size("mem")
    col_blocks = NB_DEV * lax.axis_size("clu")
    valid = (jnp.arange(slots, dtype=jnp.int32) < count).astype(jnp.float32)
    row_table = (rows[None, :] == jnp.arange(row_blocks, dtype=jnp.int32)[:, None]).astype(
        jnp.float32
    ) * valid[None, :]
    col_table = (cols[None, :] == jnp.arange(col_blocks, dtype=jnp.int32)[:, None]).astype(
        jnp.float32
    ) * valid[None, :]
    highest = lax.Precision.HIGHEST
    row_totals = jnp.sum(tiles, axis=2, dtype=jnp.float32)
    col_totals = jnp.sum(tiles, axis=1, dtype=jnp.float32)
    row_part = jnp.einsum("rt,ti->ri", row_table, row_totals, precision=highest)
    col_part = jnp.einsum("kt,tj->kj", col_table, col_totals, precision=highest)
    degree = 1.0 + spread(row_part[None], col_part[None])[0]
    inverse_root = lax.rsqrt(degree)
    classes_now = jnp.arange(CLASSES, dtype=jnp.int32)[:, None]
    labels = jnp.where(seed_class[None, :] == classes_now, seed_weight[None, :], jnp.float32(0.0))
    scores = jnp.zeros_like(labels)
    residual = labels
    direction = labels
    norm_now = squares(residual)
    for step in range(ITERS):
        width = direction.shape[0]
        scaled = (inverse_root[None, :] * direction).astype(jnp.bfloat16)
        col_panel = lax.all_gather(scaled, "clu", axis=1, tiled=True).reshape(
            width, col_blocks, side
        )
        row_panel = lax.all_gather(scaled, "mem", axis=1, tiled=True).reshape(
            width, row_blocks, side
        )
        forward = jnp.einsum(
            "tij,ctj->cti",
            tiles,
            jnp.take(col_panel, cols, axis=1),
            preferred_element_type=jnp.float32,
        )
        backward = jnp.einsum(
            "tij,cti->ctj",
            tiles,
            jnp.take(row_panel, rows, axis=1),
            preferred_element_type=jnp.float32,
        )
        row_sum = jnp.einsum("rt,cti->cri", row_table, forward, precision=highest)
        col_sum = jnp.einsum("kt,ctj->ckj", col_table, backward, precision=highest)
        image_sum = spread(row_sum, col_sum)
        image = direction - 0.99 * inverse_root[None, :] * image_sum
        alpha = norm_now / lax.psum(jnp.sum(direction * image, axis=1), ("clu", "mem"))
        scores = scores + alpha[:, None] * direction
        residual = residual - alpha[:, None] * image
        if step + 1 < ITERS:
            norm_next = squares(residual)
            direction = residual + (norm_next / norm_now)[:, None] * direction
            norm_now = norm_next
    return (scores, residual)


def solve_kernel(
    n_clu,
    n_mem,
    class_hbm,
    weight_hbm,
    tiles_hbm,
    rows_hbm,
    cols_hbm,
    count_hbm,
    scores_ref,
    residual_ref,
    class_ref,
    weight_ref,
    rows_ref,
    cols_ref,
    count_ref,
    tiles,
    turned,
    hot_rows,
    hot_cols,
    from_rows,
    from_cols,
    sums_ref,
    deg_m,
    deg_c,
    own,
    pan_m,
    pan_c,
    part_m,
    part_c,
    got_m,
    got_c,
    dots,
    dots_m,
    dots_c,
    load_sems,
    tile_sems,
    send_m,
    recv_m,
    send_c,
    recv_c,
):
    me_c = lax.axis_index("clu")
    me_m = lax.axis_index("mem")
    others_m = [None] + [lax.rem(me_m + k, n_mem) for k in range(1, n_mem)]
    others_c = [None] + [lax.rem(me_c + k, n_clu) for k in range(1, n_clu)]

    slots, side, _ = tiles.shape
    row_blocks = NB_DEV * n_mem
    col_blocks = NB_DEV * n_clu
    steps = slots // GROUP

    loads = [
        pltpu.make_async_copy(rows_hbm, rows_ref, load_sems.at[0]),
        pltpu.make_async_copy(cols_hbm, cols_ref, load_sems.at[1]),
        pltpu.make_async_copy(count_hbm, count_ref, load_sems.at[2]),
        pltpu.make_async_copy(class_hbm, class_ref, load_sems.at[3]),
        pltpu.make_async_copy(weight_hbm, weight_ref, load_sems.at[4]),
    ]

    def tile_copy(g):
        part = pl.ds(g * GROUP, GROUP)
        return pltpu.make_async_copy(tiles_hbm.at[0, 0, part], tiles.at[part], tile_sems.at[g])

    for copy in loads:
        copy.start()
    for g in range(steps):
        tile_copy(g).start()
    barrier = pltpu.get_barrier_semaphore()
    for k in range(1, n_mem):
        pl.semaphore_signal(barrier, device_id=(me_c, others_m[k]), device_id_type=MESH)
    for k in range(1, n_clu):
        pl.semaphore_signal(barrier, device_id=(others_c[k], me_m), device_id_type=MESH)

    sent = []

    def whole(room, count, send_sem, recv_sem):
        view = room.at[pl.ds(0, count - 1)]
        sent.append(pltpu.make_async_copy(view, view, send_sem))
        return pltpu.make_async_copy(view, view, recv_sem)

    def over_mem(phase, source, target, room):
        for k in range(1, n_mem):
            pltpu.make_async_remote_copy(
                src_ref=source(others_m[k]),
                dst_ref=target(k),
                send_sem=send_m.at[phase],
                recv_sem=recv_m.at[phase],
                device_id=(me_c, others_m[k]),
                device_id_type=MESH,
            ).start()
        return whole(room, n_mem, send_m.at[phase], recv_m.at[phase])

    def over_clu(phase, source, target, room):
        for k in range(1, n_clu):
            pltpu.make_async_remote_copy(
                src_ref=source(others_c[k]),
                dst_ref=target(k),
                send_sem=send_c.at[phase],
                recv_sem=recv_c.at[phase],
                device_id=(others_c[k], me_m),
                device_id_type=MESH,
            ).start()
        return whole(room, n_clu, send_c.at[phase], recv_c.at[phase])

    for copy in loads:
        copy.wait()
    count = count_ref[0, 0]
    kinds = lax.broadcasted_iota(jnp.int32, (CLASSES, weight_ref.shape[1]), 0)
    labels = jnp.where(class_ref[...] == kinds, weight_ref[...], jnp.float32(0.0))

    for blocks, hot in ((row_blocks, hot_rows), (col_blocks, hot_cols)):
        at = lax.broadcasted_iota(jnp.int32, (blocks, side), 0)
        for k in range(blocks + 1):
            hot[k] = jnp.where(at == k, jnp.float32(1.0), jnp.float32(0.0))
    from_rows[...] = jnp.zeros_like(from_rows)
    from_cols[...] = jnp.zeros_like(from_cols)

    def used(slot, block, blocks):
        unused = 1 - jnp.clip(count - slot, 0, 1)
        return block + (blocks - block) * unused

    def dot(left, held, slot):
        right = held[pl.ds(slot, PACK)].reshape(PACK * side, side)
        return lax.dot_general(
            jnp.concatenate(left, axis=1),
            right,
            (((1,), (0,)), ((), ())),
            preferred_element_type=jnp.float32,
        )

    def add_totals(g, carry):
        row_total, col_total = carry
        tile_copy(g).wait()
        for k in range(0, GROUP, PACK):
            first = g * GROUP + k
            by_row, by_col = [], []
            for slot in [first + e for e in range(PACK)]:
                row = used(slot, rows_ref[0, 0, slot], row_blocks)
                col = used(slot, cols_ref[0, 0, slot], col_blocks)
                by_row.append(hot_rows[row].astype(jnp.bfloat16))
                by_col.append(hot_cols[col].astype(jnp.bfloat16))
            col_total = col_total + dot(by_col, tiles, first)
            for e in range(0, PACK, 2):
                pair = lax.dot_general(
                    jnp.concatenate(by_row[e : e + 2], axis=0),
                    tiles[pl.ds(first + e, 2)].reshape(2 * side, side),
                    (((1,), (1,)), ((), ())),
                    preferred_element_type=jnp.float32,
                )
                row_total = row_total + pair[:row_blocks, :side] + pair[row_blocks:, side:]
        return row_total, col_total

    row_total, col_total = lax.fori_loop(
        0,
        steps,
        add_totals,
        (jnp.zeros((row_blocks, side), jnp.float32), jnp.zeros((col_blocks, side), jnp.float32)),
    )
    for k in range(row_blocks):
        at = k % NB_DEV * side
        sums_ref[k // NB_DEV, :, at : at + side] = row_total[k : k + 1]
    for k in range(col_blocks):
        at = k % NB_DEV * side
        sums_ref[n_mem + k // NB_DEV, :, at : at + side] = col_total[k : k + 1]

    def turn(g, carry):
        for slot in [g * GROUP + k for k in range(GROUP)]:
            turned[slot] = tiles[slot].T
        return carry

    def place_sums(table, held, own_ref, own_blocks, to_ref, to_blocks):
        def step(g, total):
            for k in range(0, SPAN, PACK):
                left = []
                for slot in [g * SPAN + k + e for e in range(PACK)]:
                    block = used(slot, own_ref[0, 0, slot], own_blocks)
                    start = to_blocks - 1 - to_ref[0, 0, slot]
                    panel = table[block, pl.ds(start, to_blocks)]
                    left.append(panel.reshape(to_blocks * CLASSES, side).astype(jnp.bfloat16))
                total = total + dot(left, held, g * SPAN + k)
            return total

        zero = jnp.zeros((to_blocks * CLASSES, side), jnp.float32)
        return lax.fori_loop(0, slots // SPAN, step, zero)

    def column_sums():
        return place_sums(from_rows, tiles, rows_ref, row_blocks, cols_ref, col_blocks)

    def row_sums():
        return place_sums(from_cols, turned, cols_ref, col_blocks, rows_ref, row_blocks)

    pl.semaphore_wait(barrier, n_mem + n_clu - 2)

    from_m = over_mem(0, lambda o: sums_ref.at[o], lambda k: deg_m.at[k], deg_m)
    from_c = over_clu(0, lambda o: sums_ref.at[n_mem + o], lambda k: deg_c.at[k], deg_c)
    lax.fori_loop(0, steps, turn, 0)
    degree = 1.0 + (sums_ref[me_m] + sums_ref[n_mem + me_c])
    from_m.wait()
    for k in range(1, n_mem):
        degree = degree + deg_m[k]
    from_c.wait()
    for k in range(1, n_clu):
        degree = degree + deg_c[k]
    root = lax.rsqrt(degree)

    def gather(step, panel):
        own[step] = panel
        pan_m[step, me_m] = panel
        pan_c[step, me_c] = panel
        from_m = over_mem(1 + 2 * step, lambda o: own.at[step], lambda k: pan_m.at[step, me_m], pan_m.at[step])
        from_c = over_clu(1 + 2 * step, lambda o: own.at[step], lambda k: pan_c.at[step, me_c], pan_c.at[step])
        return from_m, from_c

    def blocks_of(panels):
        for owner, panel in enumerate(panels):
            for k in range(NB_DEV):
                yield owner * NB_DEV + k, panel[:, k * side : (k + 1) * side]

    def multiply(step, from_m, from_c, between):
        phase = 2 + 2 * step
        from_m.wait()
        for k, block in blocks_of([pan_m[step, k] for k in range(n_mem)]):
            from_rows[k, col_blocks - 1] = block
        out = column_sums()
        for k in range(col_blocks):
            at = k % NB_DEV * side
            part_c[step, k // NB_DEV, :, at : at + side] = out[k * CLASSES : (k + 1) * CLASSES]
        back_c = over_clu(
            phase, lambda o: part_c.at[step, o], lambda k: got_c.at[step, k], got_c.at[step]
        )
        from_c.wait()
        panels = [pan_c[step, k] for k in range(n_clu)]
        for k, block in blocks_of(panels):
            from_cols[k, row_blocks - 1] = block
        between(panels)
        out = row_sums()
        for k in range(row_blocks):
            at = k % NB_DEV * side
            part_m[step, k // NB_DEV, :, at : at + side] = out[k * CLASSES : (k + 1) * CLASSES]
        back_m = over_mem(
            phase, lambda o: part_m.at[step, o], lambda k: got_m.at[step, k], got_m.at[step]
        )
        return back_m, back_c

    def collect(step, back_m, back_c):
        image = part_m[step, me_m] + part_c[step, me_c]
        back_c.wait()
        for k in range(1, n_clu):
            image = image + got_c[step, k]
        back_m.wait()
        for k in range(1, n_mem):
            image = image + got_m[step, k]
        return 0.99 * root * image

    from_m, from_c = gather(0, root * labels)
    back_m, back_c = multiply(0, from_m, from_c, lambda panels: None)
    first = collect(0, back_m, back_c)

    from_m, from_c = gather(1, root * first)
    lane = lax.broadcasted_iota(jnp.int32, (CLASSES, 128), 1)
    kind = lax.broadcasted_iota(jnp.int32, (CLASSES, 128), 0)
    sums = [
        jnp.sum(labels * labels, axis=1, keepdims=True),
        jnp.sum(labels * first, axis=1, keepdims=True),
        jnp.sum(first * first, axis=1, keepdims=True),
    ]
    dot_copies = []

    def send_sums(panels):
        cross = panels[0] * part_c[1, 0]
        for k in range(1, n_clu):
            cross = cross + panels[k] * part_c[1, k]
        cross = 1.98 * jnp.sum(cross, axis=1, keepdims=True)
        line = jnp.zeros((CLASSES, 128), jnp.float32)
        for k, value in enumerate([*sums, cross]):
            line = line + jnp.where(lane == kind + k * CLASSES, value, 0.0)
        dots[0] = jnp.sum(line, axis=0, keepdims=True)
        dot_copies.append(over_mem(5, lambda o: dots.at[0], lambda k: dots_m.at[k], dots_m))

    back_m, back_c = multiply(1, from_m, from_c, send_sums)
    dot_copies[0].wait()
    line = dots[0]
    for k in range(1, n_mem):
        line = line + dots_m[k]
    dots[1] = line
    dot_copies.append(over_clu(5, lambda o: dots.at[1], lambda k: dots_c.at[k], dots_c))
    second = collect(1, back_m, back_c)
    dot_copies[1].wait()
    for k in range(1, n_clu):
        line = line + dots_c[k]
    spread_line = jnp.broadcast_to(line, (CLASSES, 128))
    bb, bq, qq, qt = [
        jnp.sum(
            jnp.where(lane == kind + k * CLASSES, spread_line, 0.0), axis=1, keepdims=True
        )
        for k in range(4)
    ]
    alpha = bb / (bb - bq)
    ratio = bq / bb
    norm = alpha * alpha * (qq - ratio * bq)
    beta = norm / bb
    h = beta - alpha * ratio
    curve = alpha * alpha * (qq - qt) + 2.0 * alpha * h * (bq - qq) + h * h * (bb - bq)
    alpha_next = norm / curve
    direction = alpha * first + h * labels
    image = alpha * (first - second) + h * (labels - first)
    scores_ref[...] = alpha * labels + alpha_next * direction
    residual_ref[...] = alpha * (first - ratio * labels) - alpha_next * image

    for copy in sent:
        copy.wait()


def finish_kernel(scores_in, residual_in, scores_out, residual_out, sems):
    copies = [
        pltpu.make_async_copy(scores_in, scores_out, sems.at[0]),
        pltpu.make_async_copy(residual_in, residual_out, sems.at[1]),
    ]
    for copy in copies:
        copy.start()
    for copy in copies:
        copy.wait()


def on_device_kernel(seed_class, seed_weight, tile_values, tile_rows, tile_cols, tile_count):
    n_clu = lax.axis_size("clu")
    n_mem = lax.axis_size("mem")
    _, _, slots, side, _ = tile_values.shape
    nodes = NB_DEV * side
    row_blocks = NB_DEV * n_mem
    col_blocks = NB_DEV * n_clu
    f32 = jnp.float32
    hbm = pl.BlockSpec(memory_space=pltpu.HBM)
    vmem = pl.BlockSpec(memory_space=pltpu.VMEM)
    dma = pltpu.SemaphoreType.DMA
    panel = (CLASSES, nodes)
    results = (jax.ShapeDtypeStruct(panel, f32), jax.ShapeDtypeStruct(panel, f32))
    found = pl.pallas_call(
        functools.partial(solve_kernel, n_clu, n_mem),
        out_shape=results,
        in_specs=[hbm] * 6,
        out_specs=(vmem, vmem),
        scratch_shapes=[
            pltpu.VMEM((1, nodes), jnp.int32),
            pltpu.VMEM((1, nodes), f32),
            pltpu.SMEM(tile_rows.shape, jnp.int32),
            pltpu.SMEM(tile_cols.shape, jnp.int32),
            pltpu.SMEM(tile_count.shape, jnp.int32),
            pltpu.VMEM((slots, side, side), tile_values.dtype),
            pltpu.VMEM((slots, side, side), tile_values.dtype),
            pltpu.VMEM((row_blocks + 1, row_blocks, side), f32),
            pltpu.VMEM((col_blocks + 1, col_blocks, side), f32),
            pltpu.VMEM((row_blocks + 1, 2 * col_blocks - 1, CLASSES, side), f32),
            pltpu.VMEM((col_blocks + 1, 2 * row_blocks - 1, CLASSES, side), f32),
            pltpu.VMEM((n_mem + n_clu, 1, nodes), f32),
            pltpu.VMEM((n_mem, 1, nodes), f32),
            pltpu.VMEM((n_clu, 1, nodes), f32),
            pltpu.VMEM((ITERS, *panel), f32),
            pltpu.VMEM((ITERS, n_mem, *panel), f32),
            pltpu.VMEM((ITERS, n_clu, *panel), f32),
            pltpu.VMEM((ITERS, n_mem, *panel), f32),
            pltpu.VMEM((ITERS, n_clu, *panel), f32),
            pltpu.VMEM((ITERS, n_mem, *panel), f32),
            pltpu.VMEM((ITERS, n_clu, *panel), f32),
            pltpu.VMEM((2, 1, 128), f32),
            pltpu.VMEM((n_mem, 1, 128), f32),
            pltpu.VMEM((n_clu, 1, 128), f32),
            dma((5,)),
            dma((slots // GROUP,)),
            dma((2 + 2 * ITERS,)),
            dma((2 + 2 * ITERS,)),
            dma((2 + 2 * ITERS,)),
            dma((2 + 2 * ITERS,)),
        ],
        compiler_params=pltpu.CompilerParams(
            collective_id=0, has_side_effects=True, vmem_limit_bytes=VMEM_LIMIT
        ),
        name="solve",
    )(seed_class[None], seed_weight[None], tile_values, tile_rows, tile_cols, tile_count)
    return pl.pallas_call(
        finish_kernel,
        out_shape=results,
        in_specs=[hbm, hbm],
        out_specs=(hbm, hbm),
        scratch_shapes=[dma((2,))],
        compiler_params=pltpu.CompilerParams(vmem_limit_bytes=VMEM_LIMIT),
        name="finish",
    )(*found)


def on_device(seed_class, seed_weight, tile_values, tile_rows, tile_cols, tile_count):
    side = tile_values.shape[-1]
    blocks = NB_DEV * lax.axis_size("mem") * NB_DEV * lax.axis_size("clu")
    if blocks * CLASSES * side * 16 <= TABLE_LIMIT:
        run = on_device_kernel
    else:
        run = on_device_slots
    return run(seed_class, seed_weight, tile_values, tile_rows, tile_cols, tile_count)


def solution(mesh):
    in_specs = (
        P(("clu", "mem")),
        P(("clu", "mem")),
        P("clu", "mem", None, None, None),
        P("clu", "mem", None),
        P("clu", "mem", None),
        P("clu", "mem"),
    )
    out_specs = (P(None, ("clu", "mem")), P(None, ("clu", "mem")))
    return jax.shard_map(
        on_device, mesh=mesh, in_specs=in_specs, out_specs=out_specs, check_vma=False
    )
```

```python
import functools
import jax
import jax.numpy as jnp
from jax import lax
from jax.experimental import pallas as pl
from jax.experimental.pallas import tpu as pltpu
from jax.sharding import PartitionSpec as P

CLASSES = 8
NB_DEV = 2
ITERS = 2
GROUP = 16
SPAN = 96
PACK = 4
TABLE_LIMIT = 16 * 1024 * 1024
VMEM_LIMIT = 64 * 1024 * 1024
MESH = pl.DeviceIdType.MESH


def spread(row_part, col_part):
    width = row_part.shape[0]
    from_rows = lax.psum_scatter(
        row_part.reshape(width, -1), "mem", scatter_dimension=1, tiled=True
    )
    from_cols = lax.psum_scatter(
        col_part.reshape(width, -1), "clu", scatter_dimension=1, tiled=True
    )
    return from_rows + from_cols


def squares(residual):
    return lax.psum(jnp.sum(residual * residual, axis=1), ("clu", "mem"))


def on_device_slots(seed_class, seed_weight, tile_values, tile_rows, tile_cols, tile_count):
    tiles = tile_values[0, 0]
    rows = tile_rows[0, 0]
    cols = tile_cols[0, 0]
    count = tile_count[0, 0]
    slots = tiles.shape[0]
    side = tiles.shape[1]
    row_blocks = NB_DEV * lax.axis_size("mem")
    col_blocks = NB_DEV * lax.axis_size("clu")
    valid = (jnp.arange(slots, dtype=jnp.int32) < count).astype(jnp.float32)
    row_table = (rows[None, :] == jnp.arange(row_blocks, dtype=jnp.int32)[:, None]).astype(
        jnp.float32
    ) * valid[None, :]
    col_table = (cols[None, :] == jnp.arange(col_blocks, dtype=jnp.int32)[:, None]).astype(
        jnp.float32
    ) * valid[None, :]
    highest = lax.Precision.HIGHEST
    row_totals = jnp.sum(tiles, axis=2, dtype=jnp.float32)
    col_totals = jnp.sum(tiles, axis=1, dtype=jnp.float32)
    row_part = jnp.einsum("rt,ti->ri", row_table, row_totals, precision=highest)
    col_part = jnp.einsum("kt,tj->kj", col_table, col_totals, precision=highest)
    degree = 1.0 + spread(row_part[None], col_part[None])[0]
    inverse_root = lax.rsqrt(degree)
    classes_now = jnp.arange(CLASSES, dtype=jnp.int32)[:, None]
    labels = jnp.where(seed_class[None, :] == classes_now, seed_weight[None, :], jnp.float32(0.0))
    scores = jnp.zeros_like(labels)
    residual = labels
    direction = labels
    norm_now = squares(residual)
    for step in range(ITERS):
        width = direction.shape[0]
        scaled = (inverse_root[None, :] * direction).astype(jnp.bfloat16)
        col_panel = lax.all_gather(scaled, "clu", axis=1, tiled=True).reshape(
            width, col_blocks, side
        )
        row_panel = lax.all_gather(scaled, "mem", axis=1, tiled=True).reshape(
            width, row_blocks, side
        )
        forward = jnp.einsum(
            "tij,ctj->cti",
            tiles,
            jnp.take(col_panel, cols, axis=1),
            preferred_element_type=jnp.float32,
        )
        backward = jnp.einsum(
            "tij,cti->ctj",
            tiles,
            jnp.take(row_panel, rows, axis=1),
            preferred_element_type=jnp.float32,
        )
        row_sum = jnp.einsum("rt,cti->cri", row_table, forward, precision=highest)
        col_sum = jnp.einsum("kt,ctj->ckj", col_table, backward, precision=highest)
        image_sum = spread(row_sum, col_sum)
        image = direction - 0.99 * inverse_root[None, :] * image_sum
        alpha = norm_now / lax.psum(jnp.sum(direction * image, axis=1), ("clu", "mem"))
        scores = scores + alpha[:, None] * direction
        residual = residual - alpha[:, None] * image
        if step + 1 < ITERS:
            norm_next = squares(residual)
            direction = residual + (norm_next / norm_now)[:, None] * direction
            norm_now = norm_next
    return (scores, residual)


def solve_kernel(
    n_clu,
    n_mem,
    class_hbm,
    weight_hbm,
    tiles_hbm,
    rows_hbm,
    cols_hbm,
    count_hbm,
    scores_ref,
    residual_ref,
    class_ref,
    weight_ref,
    rows_ref,
    cols_ref,
    count_ref,
    tiles,
    turned,
    hot_rows,
    hot_cols,
    from_rows,
    from_cols,
    sums_ref,
    deg_m,
    deg_c,
    own,
    pan_m,
    pan_c,
    part_m,
    part_c,
    got_m,
    got_c,
    dots,
    dots_m,
    dots_c,
    load_sems,
    tile_sems,
    send_m,
    recv_m,
    send_c,
    recv_c,
):
    me_c = lax.axis_index("clu")
    me_m = lax.axis_index("mem")
    others_m = [None] + [lax.rem(me_m + k, n_mem) for k in range(1, n_mem)]
    others_c = [None] + [lax.rem(me_c + k, n_clu) for k in range(1, n_clu)]

    slots, side, _ = tiles.shape
    row_blocks = NB_DEV * n_mem
    col_blocks = NB_DEV * n_clu
    steps = slots // GROUP

    loads = [
        pltpu.make_async_copy(rows_hbm, rows_ref, load_sems.at[0]),
        pltpu.make_async_copy(cols_hbm, cols_ref, load_sems.at[1]),
        pltpu.make_async_copy(count_hbm, count_ref, load_sems.at[2]),
        pltpu.make_async_copy(class_hbm, class_ref, load_sems.at[3]),
        pltpu.make_async_copy(weight_hbm, weight_ref, load_sems.at[4]),
    ]

    def tile_copy(g):
        part = pl.ds(g * GROUP, GROUP)
        return pltpu.make_async_copy(tiles_hbm.at[0, 0, part], tiles.at[part], tile_sems.at[g])

    for copy in loads:
        copy.start()
    for g in range(steps):
        tile_copy(g).start()
    barrier = pltpu.get_barrier_semaphore()
    for k in range(1, n_mem):
        pl.semaphore_signal(barrier, device_id=(me_c, others_m[k]), device_id_type=MESH)
    for k in range(1, n_clu):
        pl.semaphore_signal(barrier, device_id=(others_c[k], me_m), device_id_type=MESH)

    sent = []

    def whole(room, count, send_sem, recv_sem):
        view = room.at[pl.ds(0, count - 1)]
        sent.append(pltpu.make_async_copy(view, view, send_sem))
        return pltpu.make_async_copy(view, view, recv_sem)

    def over_mem(phase, source, target, room):
        for k in range(1, n_mem):
            pltpu.make_async_remote_copy(
                src_ref=source(others_m[k]),
                dst_ref=target(k),
                send_sem=send_m.at[phase],
                recv_sem=recv_m.at[phase],
                device_id=(me_c, others_m[k]),
                device_id_type=MESH,
            ).start()
        return whole(room, n_mem, send_m.at[phase], recv_m.at[phase])

    def over_clu(phase, source, target, room):
        for k in range(1, n_clu):
            pltpu.make_async_remote_copy(
                src_ref=source(others_c[k]),
                dst_ref=target(k),
                send_sem=send_c.at[phase],
                recv_sem=recv_c.at[phase],
                device_id=(others_c[k], me_m),
                device_id_type=MESH,
            ).start()
        return whole(room, n_clu, send_c.at[phase], recv_c.at[phase])

    for copy in loads:
        copy.wait()
    count = count_ref[0, 0]
    kinds = lax.broadcasted_iota(jnp.int32, (CLASSES, weight_ref.shape[1]), 0)
    labels = jnp.where(class_ref[...] == kinds, weight_ref[...], jnp.float32(0.0))

    for blocks, hot in ((row_blocks, hot_rows), (col_blocks, hot_cols)):
        at = lax.broadcasted_iota(jnp.int32, (blocks, side), 0)
        for k in range(blocks + 1):
            hot[k] = jnp.where(at == k, jnp.float32(1.0), jnp.float32(0.0))
    from_rows[...] = jnp.zeros_like(from_rows)
    from_cols[...] = jnp.zeros_like(from_cols)

    def used(slot, block, blocks):
        unused = 1 - jnp.clip(count - slot, 0, 1)
        return block + (blocks - block) * unused

    def dot(left, held, slot):
        right = held[pl.ds(slot, PACK)].reshape(PACK * side, side)
        return lax.dot_general(
            jnp.concatenate(left, axis=1),
            right,
            (((1,), (0,)), ((), ())),
            preferred_element_type=jnp.float32,
        )

    def add_totals(g, carry):
        row_total, col_total = carry
        tile_copy(g).wait()
        for k in range(0, GROUP, PACK):
            first = g * GROUP + k
            by_row, by_col = [], []
            for slot in [first + e for e in range(PACK)]:
                row = used(slot, rows_ref[0, 0, slot], row_blocks)
                col = used(slot, cols_ref[0, 0, slot], col_blocks)
                by_row.append(hot_rows[row].astype(jnp.bfloat16))
                by_col.append(hot_cols[col].astype(jnp.bfloat16))
            col_total = col_total + dot(by_col, tiles, first)
            for e in range(0, PACK, 2):
                pair = lax.dot_general(
                    jnp.concatenate(by_row[e : e + 2], axis=0),
                    tiles[pl.ds(first + e, 2)].reshape(2 * side, side),
                    (((1,), (1,)), ((), ())),
                    preferred_element_type=jnp.float32,
                )
                row_total = row_total + pair[:row_blocks, :side] + pair[row_blocks:, side:]
        return row_total, col_total

    row_total, col_total = lax.fori_loop(
        0,
        steps,
        add_totals,
        (jnp.zeros((row_blocks, side), jnp.float32), jnp.zeros((col_blocks, side), jnp.float32)),
    )
    for k in range(row_blocks):
        at = k % NB_DEV * side
        sums_ref[k // NB_DEV, :, at : at + side] = row_total[k : k + 1]
    for k in range(col_blocks):
        at = k % NB_DEV * side
        sums_ref[n_mem + k // NB_DEV, :, at : at + side] = col_total[k : k + 1]

    def turn(g, carry):
        for slot in [g * GROUP + k for k in range(GROUP)]:
            turned[slot] = tiles[slot].T
        return carry

    def place_sums(table, held, own_ref, own_blocks, to_ref, to_blocks):
        def step(g, total):
            for k in range(0, SPAN, PACK):
                left = []
                for slot in [g * SPAN + k + e for e in range(PACK)]:
                    block = used(slot, own_ref[0, 0, slot], own_blocks)
                    start = to_blocks - 1 - to_ref[0, 0, slot]
                    panel = table[block, pl.ds(start, to_blocks)]
                    left.append(panel.reshape(to_blocks * CLASSES, side).astype(jnp.bfloat16))
                total = total + dot(left, held, g * SPAN + k)
            return total

        zero = jnp.zeros((to_blocks * CLASSES, side), jnp.float32)
        return lax.fori_loop(0, slots // SPAN, step, zero)

    def column_sums():
        return place_sums(from_rows, tiles, rows_ref, row_blocks, cols_ref, col_blocks)

    def row_sums():
        return place_sums(from_cols, turned, cols_ref, col_blocks, rows_ref, row_blocks)

    pl.semaphore_wait(barrier, n_mem + n_clu - 2)

    from_m = over_mem(0, lambda o: sums_ref.at[o], lambda k: deg_m.at[k], deg_m)
    from_c = over_clu(0, lambda o: sums_ref.at[n_mem + o], lambda k: deg_c.at[k], deg_c)
    lax.fori_loop(0, steps // 2, turn, 0)
    degree = 1.0 + (sums_ref[me_m] + sums_ref[n_mem + me_c])
    from_m.wait()
    for k in range(1, n_mem):
        degree = degree + deg_m[k]
    from_c.wait()
    for k in range(1, n_clu):
        degree = degree + deg_c[k]
    root = lax.rsqrt(degree)

    def gather(step, panel):
        panel = jnp.concatenate(
            [panel[:, k * side : (k + 1) * side] for k in range(NB_DEV)], axis=0
        ).astype(jnp.bfloat16)
        own[step] = panel
        pan_m[step, me_m] = panel
        pan_c[step, me_c] = panel
        from_m = over_mem(1 + 2 * step, lambda o: own.at[step], lambda k: pan_m.at[step, me_m], pan_m.at[step])
        from_c = over_clu(1 + 2 * step, lambda o: own.at[step], lambda k: pan_c.at[step, me_c], pan_c.at[step])
        return from_m, from_c

    def multiply(step, from_m, from_c, between):
        phase = 2 + 2 * step
        from_m.wait()
        for k in range(n_mem):
            panel = pan_m[step, k].astype(jnp.float32).reshape(NB_DEV, CLASSES, side)
            for e in range(NB_DEV):
                from_rows[k * NB_DEV + e, col_blocks - 1] = panel[e]
        out = column_sums()
        for k in range(col_blocks):
            at = k % NB_DEV * side
            part_c[step, k // NB_DEV, :, at : at + side] = out[k * CLASSES : (k + 1) * CLASSES]
        back_c = over_clu(
            phase, lambda o: part_c.at[step, o], lambda k: got_c.at[step, k], got_c.at[step]
        )
        from_c.wait()
        blocks = []
        for k in range(n_clu):
            panel = pan_c[step, k].astype(jnp.float32).reshape(NB_DEV, CLASSES, side)
            for e in range(NB_DEV):
                blocks.append(panel[e])
                from_cols[k * NB_DEV + e, row_blocks - 1] = panel[e]
        between(blocks, out)
        out = row_sums()
        for k in range(row_blocks):
            at = k % NB_DEV * side
            part_m[step, k // NB_DEV, :, at : at + side] = out[k * CLASSES : (k + 1) * CLASSES]
        back_m = over_mem(
            phase, lambda o: part_m.at[step, o], lambda k: got_m.at[step, k], got_m.at[step]
        )
        return back_m, back_c

    def collect(step, back_m, back_c):
        image = part_m[step, me_m] + part_c[step, me_c]
        back_c.wait()
        for k in range(1, n_clu):
            image = image + got_c[step, k]
        back_m.wait()
        for k in range(1, n_mem):
            image = image + got_m[step, k]
        return 0.99 * root * image

    from_m, from_c = gather(0, root * labels)
    lax.fori_loop(steps // 2, steps, turn, 0)
    back_m, back_c = multiply(0, from_m, from_c, lambda blocks, out: None)
    first = collect(0, back_m, back_c)

    from_m, from_c = gather(1, root * first)
    lane = lax.broadcasted_iota(jnp.int32, (CLASSES, 128), 1)
    kind = lax.broadcasted_iota(jnp.int32, (CLASSES, 128), 0)
    sums = [
        jnp.sum(labels * labels, axis=1, keepdims=True),
        jnp.sum(labels * first, axis=1, keepdims=True),
        jnp.sum(first * first, axis=1, keepdims=True),
    ]
    dot_copies = []

    def send_sums(blocks, out):
        cross = jnp.zeros((CLASSES, side), jnp.float32)
        for k, block in enumerate(blocks):
            cross = cross + block * out[k * CLASSES : (k + 1) * CLASSES]
        cross = 1.98 * jnp.sum(cross, axis=1, keepdims=True)
        line = jnp.zeros((CLASSES, 128), jnp.float32)
        for k, value in enumerate([*sums, cross]):
            line = line + jnp.where(lane == kind + k * CLASSES, value, 0.0)
        dots[0] = jnp.sum(line, axis=0, keepdims=True)
        dot_copies.append(over_mem(5, lambda o: dots.at[0], lambda k: dots_m.at[k], dots_m))

    back_m, back_c = multiply(1, from_m, from_c, send_sums)
    dot_copies[0].wait()
    line = dots[0]
    for k in range(1, n_mem):
        line = line + dots_m[k]
    dots[1] = line
    dot_copies.append(over_clu(5, lambda o: dots.at[1], lambda k: dots_c.at[k], dots_c))
    second = collect(1, back_m, back_c)
    dot_copies[1].wait()
    for k in range(1, n_clu):
        line = line + dots_c[k]
    spread_line = jnp.broadcast_to(line, (CLASSES, 128))
    bb, bq, qq, qt = [
        jnp.sum(
            jnp.where(lane == kind + k * CLASSES, spread_line, 0.0), axis=1, keepdims=True
        )
        for k in range(4)
    ]
    alpha = bb / (bb - bq)
    ratio = bq / bb
    norm = alpha * alpha * (qq - ratio * bq)
    beta = norm / bb
    h = beta - alpha * ratio
    curve = alpha * alpha * (qq - qt) + 2.0 * alpha * h * (bq - qq) + h * h * (bb - bq)
    alpha_next = norm / curve
    direction = alpha * first + h * labels
    image = alpha * (first - second) + h * (labels - first)
    scores_ref[...] = alpha * labels + alpha_next * direction
    residual_ref[...] = alpha * (first - ratio * labels) - alpha_next * image

    for copy in sent:
        copy.wait()


def finish_kernel(scores_in, residual_in, scores_out, residual_out, sems):
    copies = [
        pltpu.make_async_copy(scores_in, scores_out, sems.at[0]),
        pltpu.make_async_copy(residual_in, residual_out, sems.at[1]),
    ]
    for copy in copies:
        copy.start()
    for copy in copies:
        copy.wait()


def on_device_kernel(seed_class, seed_weight, tile_values, tile_rows, tile_cols, tile_count):
    n_clu = lax.axis_size("clu")
    n_mem = lax.axis_size("mem")
    _, _, slots, side, _ = tile_values.shape
    nodes = NB_DEV * side
    row_blocks = NB_DEV * n_mem
    col_blocks = NB_DEV * n_clu
    f32 = jnp.float32
    hbm = pl.BlockSpec(memory_space=pltpu.HBM)
    vmem = pl.BlockSpec(memory_space=pltpu.VMEM)
    dma = pltpu.SemaphoreType.DMA
    panel = (CLASSES, nodes)
    sent = (NB_DEV * CLASSES, side)
    results = (jax.ShapeDtypeStruct(panel, f32), jax.ShapeDtypeStruct(panel, f32))
    found = pl.pallas_call(
        functools.partial(solve_kernel, n_clu, n_mem),
        out_shape=results,
        in_specs=[hbm] * 6,
        out_specs=(vmem, vmem),
        scratch_shapes=[
            pltpu.VMEM((1, nodes), jnp.int32),
            pltpu.VMEM((1, nodes), f32),
            pltpu.SMEM(tile_rows.shape, jnp.int32),
            pltpu.SMEM(tile_cols.shape, jnp.int32),
            pltpu.SMEM(tile_count.shape, jnp.int32),
            pltpu.VMEM((slots, side, side), tile_values.dtype),
            pltpu.VMEM((slots, side, side), tile_values.dtype),
            pltpu.VMEM((row_blocks + 1, row_blocks, side), f32),
            pltpu.VMEM((col_blocks + 1, col_blocks, side), f32),
            pltpu.VMEM((row_blocks + 1, 2 * col_blocks - 1, CLASSES, side), f32),
            pltpu.VMEM((col_blocks + 1, 2 * row_blocks - 1, CLASSES, side), f32),
            pltpu.VMEM((n_mem + n_clu, 1, nodes), f32),
            pltpu.VMEM((n_mem, 1, nodes), f32),
            pltpu.VMEM((n_clu, 1, nodes), f32),
            pltpu.VMEM((ITERS, *sent), jnp.bfloat16),
            pltpu.VMEM((ITERS, n_mem, *sent), jnp.bfloat16),
            pltpu.VMEM((ITERS, n_clu, *sent), jnp.bfloat16),
            pltpu.VMEM((ITERS, n_mem, *panel), f32),
            pltpu.VMEM((ITERS, n_clu, *panel), f32),
            pltpu.VMEM((ITERS, n_mem, *panel), f32),
            pltpu.VMEM((ITERS, n_clu, *panel), f32),
            pltpu.VMEM((2, 1, 128), f32),
            pltpu.VMEM((n_mem, 1, 128), f32),
            pltpu.VMEM((n_clu, 1, 128), f32),
            dma((5,)),
            dma((slots // GROUP,)),
            dma((2 + 2 * ITERS,)),
            dma((2 + 2 * ITERS,)),
            dma((2 + 2 * ITERS,)),
            dma((2 + 2 * ITERS,)),
        ],
        compiler_params=pltpu.CompilerParams(
            collective_id=0, has_side_effects=True, vmem_limit_bytes=VMEM_LIMIT
        ),
        name="solve",
    )(seed_class[None], seed_weight[None], tile_values, tile_rows, tile_cols, tile_count)
    return pl.pallas_call(
        finish_kernel,
        out_shape=results,
        in_specs=[hbm, hbm],
        out_specs=(hbm, hbm),
        scratch_shapes=[dma((2,))],
        compiler_params=pltpu.CompilerParams(vmem_limit_bytes=VMEM_LIMIT),
        name="finish",
    )(*found)


def on_device(seed_class, seed_weight, tile_values, tile_rows, tile_cols, tile_count):
    side = tile_values.shape[-1]
    blocks = NB_DEV * lax.axis_size("mem") * NB_DEV * lax.axis_size("clu")
    if blocks * CLASSES * side * 16 <= TABLE_LIMIT:
        run = on_device_kernel
    else:
        run = on_device_slots
    return run(seed_class, seed_weight, tile_values, tile_rows, tile_cols, tile_count)


def solution(mesh):
    in_specs = (
        P(("clu", "mem")),
        P(("clu", "mem")),
        P("clu", "mem", None, None, None),
        P("clu", "mem", None),
        P("clu", "mem", None),
        P("clu", "mem"),
    )
    out_specs = (P(None, ("clu", "mem")), P(None, ("clu", "mem")))
    return jax.shard_map(
        on_device, mesh=mesh, in_specs=in_specs, out_specs=out_specs, check_vma=False
    )
```

```python
import functools
import jax
import jax.numpy as jnp
from jax import lax
from jax.experimental import pallas as pl
from jax.experimental.pallas import tpu as pltpu
from jax.sharding import PartitionSpec as P

CLASSES = 8
NB_DEV = 2
ITERS = 2
GROUP = 16
SPAN = 96
PACK = 4
TABLE_LIMIT = 16 * 1024 * 1024
VMEM_LIMIT = 64 * 1024 * 1024
MESH = pl.DeviceIdType.MESH


def spread(row_part, col_part):
    width = row_part.shape[0]
    from_rows = lax.psum_scatter(
        row_part.reshape(width, -1), "mem", scatter_dimension=1, tiled=True
    )
    from_cols = lax.psum_scatter(
        col_part.reshape(width, -1), "clu", scatter_dimension=1, tiled=True
    )
    return from_rows + from_cols


def squares(residual):
    return lax.psum(jnp.sum(residual * residual, axis=1), ("clu", "mem"))


def on_device_slots(seed_class, seed_weight, tile_values, tile_rows, tile_cols, tile_count):
    tiles = tile_values[0, 0]
    rows = tile_rows[0, 0]
    cols = tile_cols[0, 0]
    count = tile_count[0, 0]
    slots = tiles.shape[0]
    side = tiles.shape[1]
    row_blocks = NB_DEV * lax.axis_size("mem")
    col_blocks = NB_DEV * lax.axis_size("clu")
    valid = (jnp.arange(slots, dtype=jnp.int32) < count).astype(jnp.float32)
    row_table = (rows[None, :] == jnp.arange(row_blocks, dtype=jnp.int32)[:, None]).astype(
        jnp.float32
    ) * valid[None, :]
    col_table = (cols[None, :] == jnp.arange(col_blocks, dtype=jnp.int32)[:, None]).astype(
        jnp.float32
    ) * valid[None, :]
    highest = lax.Precision.HIGHEST
    row_totals = jnp.sum(tiles, axis=2, dtype=jnp.float32)
    col_totals = jnp.sum(tiles, axis=1, dtype=jnp.float32)
    row_part = jnp.einsum("rt,ti->ri", row_table, row_totals, precision=highest)
    col_part = jnp.einsum("kt,tj->kj", col_table, col_totals, precision=highest)
    degree = 1.0 + spread(row_part[None], col_part[None])[0]
    inverse_root = lax.rsqrt(degree)
    classes_now = jnp.arange(CLASSES, dtype=jnp.int32)[:, None]
    labels = jnp.where(seed_class[None, :] == classes_now, seed_weight[None, :], jnp.float32(0.0))
    scores = jnp.zeros_like(labels)
    residual = labels
    direction = labels
    norm_now = squares(residual)
    for step in range(ITERS):
        width = direction.shape[0]
        scaled = (inverse_root[None, :] * direction).astype(jnp.bfloat16)
        col_panel = lax.all_gather(scaled, "clu", axis=1, tiled=True).reshape(
            width, col_blocks, side
        )
        row_panel = lax.all_gather(scaled, "mem", axis=1, tiled=True).reshape(
            width, row_blocks, side
        )
        forward = jnp.einsum(
            "tij,ctj->cti",
            tiles,
            jnp.take(col_panel, cols, axis=1),
            preferred_element_type=jnp.float32,
        )
        backward = jnp.einsum(
            "tij,cti->ctj",
            tiles,
            jnp.take(row_panel, rows, axis=1),
            preferred_element_type=jnp.float32,
        )
        row_sum = jnp.einsum("rt,cti->cri", row_table, forward, precision=highest)
        col_sum = jnp.einsum("kt,ctj->ckj", col_table, backward, precision=highest)
        image_sum = spread(row_sum, col_sum)
        image = direction - 0.99 * inverse_root[None, :] * image_sum
        alpha = norm_now / lax.psum(jnp.sum(direction * image, axis=1), ("clu", "mem"))
        scores = scores + alpha[:, None] * direction
        residual = residual - alpha[:, None] * image
        if step + 1 < ITERS:
            norm_next = squares(residual)
            direction = residual + (norm_next / norm_now)[:, None] * direction
            norm_now = norm_next
    return (scores, residual)


def solve_kernel(
    n_clu,
    n_mem,
    class_hbm,
    weight_hbm,
    tiles_hbm,
    rows_hbm,
    cols_hbm,
    count_hbm,
    scores_ref,
    residual_ref,
    class_ref,
    weight_ref,
    rows_ref,
    cols_ref,
    count_ref,
    tiles,
    turned,
    hot_rows,
    hot_cols,
    from_rows,
    from_cols,
    sums_ref,
    deg_m,
    deg_c,
    own,
    pan_m,
    pan_c,
    part_m,
    part_c,
    got_m,
    got_c,
    dots,
    dots_m,
    dots_c,
    load_sems,
    tile_sems,
    send_m,
    recv_m,
    send_c,
    recv_c,
):
    me_c = lax.axis_index("clu")
    me_m = lax.axis_index("mem")
    others_m = [None] + [lax.rem(me_m + k, n_mem) for k in range(1, n_mem)]
    others_c = [None] + [lax.rem(me_c + k, n_clu) for k in range(1, n_clu)]

    slots, side, _ = tiles.shape
    row_blocks = NB_DEV * n_mem
    col_blocks = NB_DEV * n_clu
    steps = slots // GROUP

    loads = [
        pltpu.make_async_copy(rows_hbm, rows_ref, load_sems.at[0]),
        pltpu.make_async_copy(cols_hbm, cols_ref, load_sems.at[1]),
        pltpu.make_async_copy(count_hbm, count_ref, load_sems.at[2]),
        pltpu.make_async_copy(class_hbm, class_ref, load_sems.at[3]),
        pltpu.make_async_copy(weight_hbm, weight_ref, load_sems.at[4]),
    ]

    def tile_copy(g):
        part = pl.ds(g * GROUP, GROUP)
        return pltpu.make_async_copy(tiles_hbm.at[0, 0, part], tiles.at[part], tile_sems.at[g])

    for copy in loads:
        copy.start()
    for g in range(steps):
        tile_copy(g).start()
    barrier = pltpu.get_barrier_semaphore()
    for k in range(1, n_mem):
        pl.semaphore_signal(barrier, device_id=(me_c, others_m[k]), device_id_type=MESH)
    for k in range(1, n_clu):
        pl.semaphore_signal(barrier, device_id=(others_c[k], me_m), device_id_type=MESH)

    sent = []

    def whole(room, count, send_sem, recv_sem):
        view = room.at[pl.ds(0, count - 1)]
        sent.append(pltpu.make_async_copy(view, view, send_sem))
        return pltpu.make_async_copy(view, view, recv_sem)

    def over_mem(phase, source, target, room):
        for k in range(1, n_mem):
            pltpu.make_async_remote_copy(
                src_ref=source(others_m[k]),
                dst_ref=target(k),
                send_sem=send_m.at[phase],
                recv_sem=recv_m.at[phase],
                device_id=(me_c, others_m[k]),
                device_id_type=MESH,
            ).start()
        return whole(room, n_mem, send_m.at[phase], recv_m.at[phase])

    def over_clu(phase, source, target, room):
        for k in range(1, n_clu):
            pltpu.make_async_remote_copy(
                src_ref=source(others_c[k]),
                dst_ref=target(k),
                send_sem=send_c.at[phase],
                recv_sem=recv_c.at[phase],
                device_id=(others_c[k], me_m),
                device_id_type=MESH,
            ).start()
        return whole(room, n_clu, send_c.at[phase], recv_c.at[phase])

    for copy in loads:
        copy.wait()
    count = count_ref[0, 0]
    kinds = lax.broadcasted_iota(jnp.int32, (CLASSES, weight_ref.shape[1]), 0)
    labels = jnp.where(class_ref[...] == kinds, weight_ref[...], jnp.float32(0.0))

    for blocks, hot in ((row_blocks, hot_rows), (col_blocks, hot_cols)):
        at = lax.broadcasted_iota(jnp.int32, (blocks, side), 0)
        for k in range(blocks + 1):
            hot[k] = jnp.where(at == k, jnp.float32(1.0), jnp.float32(0.0))
    from_rows[...] = jnp.zeros_like(from_rows)
    from_cols[...] = jnp.zeros_like(from_cols)

    def used(slot, block, blocks):
        unused = 1 - jnp.clip(count - slot, 0, 1)
        return block + (blocks - block) * unused

    def dot(left, held, slot):
        right = held[pl.ds(slot, PACK)].reshape(PACK * side, side)
        return lax.dot_general(
            jnp.concatenate(left, axis=1),
            right,
            (((1,), (0,)), ((), ())),
            preferred_element_type=jnp.float32,
        )

    def add_totals(g, carry):
        row_total, col_total = carry
        tile_copy(g).wait()
        for k in range(0, GROUP, PACK):
            first = g * GROUP + k
            by_row, by_col = [], []
            for slot in [first + e for e in range(PACK)]:
                row = used(slot, rows_ref[0, 0, slot], row_blocks)
                col = used(slot, cols_ref[0, 0, slot], col_blocks)
                by_row.append(hot_rows[row].astype(jnp.bfloat16))
                by_col.append(hot_cols[col].astype(jnp.bfloat16))
            col_total = col_total + dot(by_col, tiles, first)
            for e in range(0, PACK, 2):
                pair = lax.dot_general(
                    jnp.concatenate(by_row[e : e + 2], axis=0),
                    tiles[pl.ds(first + e, 2)].reshape(2 * side, side),
                    (((1,), (1,)), ((), ())),
                    preferred_element_type=jnp.float32,
                )
                row_total = row_total + pair[:row_blocks, :side] + pair[row_blocks:, side:]
        return row_total, col_total

    row_total, col_total = lax.fori_loop(
        0,
        steps,
        add_totals,
        (jnp.zeros((row_blocks, side), jnp.float32), jnp.zeros((col_blocks, side), jnp.float32)),
    )
    for k in range(row_blocks):
        at = k % NB_DEV * side
        sums_ref[k // NB_DEV, :, at : at + side] = row_total[k : k + 1]
    for k in range(col_blocks):
        at = k % NB_DEV * side
        sums_ref[n_mem + k // NB_DEV, :, at : at + side] = col_total[k : k + 1]

    def turn(g, carry):
        for slot in [g * GROUP + k for k in range(GROUP)]:
            turned[slot] = tiles[slot].T
        return carry

    def place_sums(table, held, own_ref, own_blocks, to_ref, to_blocks):
        def step(g, total):
            for k in range(0, SPAN, PACK):
                left = []
                for slot in [g * SPAN + k + e for e in range(PACK)]:
                    block = used(slot, own_ref[0, 0, slot], own_blocks)
                    start = to_blocks - 1 - to_ref[0, 0, slot]
                    panel = table[block, pl.ds(start, to_blocks)]
                    left.append(panel.reshape(to_blocks * CLASSES, side).astype(jnp.bfloat16))
                total = total + dot(left, held, g * SPAN + k)
            return total

        zero = jnp.zeros((to_blocks * CLASSES, side), jnp.float32)
        return lax.fori_loop(0, slots // SPAN, step, zero)

    def column_sums():
        return place_sums(from_rows, tiles, rows_ref, row_blocks, cols_ref, col_blocks)

    def row_sums():
        return place_sums(from_cols, turned, cols_ref, col_blocks, rows_ref, row_blocks)

    pl.semaphore_wait(barrier, n_mem + n_clu - 2)

    from_m = over_mem(0, lambda o: sums_ref.at[o], lambda k: deg_m.at[k], deg_m)
    from_c = over_clu(0, lambda o: sums_ref.at[n_mem + o], lambda k: deg_c.at[k], deg_c)
    lax.fori_loop(0, steps // 2, turn, 0)
    degree = 1.0 + (sums_ref[me_m] + sums_ref[n_mem + me_c])
    from_m.wait()
    for k in range(1, n_mem):
        degree = degree + deg_m[k]
    from_c.wait()
    for k in range(1, n_clu):
        degree = degree + deg_c[k]
    root = lax.rsqrt(degree)

    def gather(step, panel):
        panel = jnp.concatenate(
            [panel[:, k * side : (k + 1) * side] for k in range(NB_DEV)], axis=0
        ).astype(jnp.bfloat16)
        own[step] = panel
        pan_m[step, me_m] = panel
        pan_c[step, me_c] = panel
        from_m = over_mem(1 + 2 * step, lambda o: own.at[step], lambda k: pan_m.at[step, me_m], pan_m.at[step])
        from_c = over_clu(1 + 2 * step, lambda o: own.at[step], lambda k: pan_c.at[step, me_c], pan_c.at[step])
        return from_m, from_c

    def place_panels(panels, count, table, at):
        blocks = []
        for k in range(count):
            panel = panels[k].astype(jnp.float32).reshape(NB_DEV, CLASSES, side)
            for e in range(NB_DEV):
                blocks.append(panel[e])
                table[k * NB_DEV + e, at] = panel[e]
        return blocks

    def parts_of(out, parts, blocks):
        for k in range(blocks):
            at = k % NB_DEV * side
            parts[k // NB_DEV, :, at : at + side] = out[k * CLASSES : (k + 1) * CLASSES]

    def multiply(step, from_m, from_c, between):
        phase = 2 + 2 * step
        from_c.wait()
        place_panels(pan_c.at[step], n_clu, from_cols, row_blocks - 1)
        out = row_sums()
        parts_of(out, part_m.at[step], row_blocks)
        back_m = over_mem(
            phase, lambda o: part_m.at[step, o], lambda k: got_m.at[step, k], got_m.at[step]
        )
        from_m.wait()
        between(place_panels(pan_m.at[step], n_mem, from_rows, col_blocks - 1), out)
        parts_of(column_sums(), part_c.at[step], col_blocks)
        back_c = over_clu(
            phase, lambda o: part_c.at[step, o], lambda k: got_c.at[step, k], got_c.at[step]
        )
        return back_m, back_c

    def collect(step, back_m, back_c):
        image = part_m[step, me_m] + part_c[step, me_c]
        back_m.wait()
        for k in range(1, n_mem):
            image = image + got_m[step, k]
        back_c.wait()
        for k in range(1, n_clu):
            image = image + got_c[step, k]
        return 0.99 * root * image

    from_m, from_c = gather(0, root * labels)
    lax.fori_loop(steps // 2, steps, turn, 0)
    back_m, back_c = multiply(0, from_m, from_c, lambda blocks, out: None)
    first = collect(0, back_m, back_c)

    from_m, from_c = gather(1, root * first)
    lane = lax.broadcasted_iota(jnp.int32, (CLASSES, 128), 1)
    kind = lax.broadcasted_iota(jnp.int32, (CLASSES, 128), 0)
    sums = [
        jnp.sum(labels * labels, axis=1, keepdims=True),
        jnp.sum(labels * first, axis=1, keepdims=True),
        jnp.sum(first * first, axis=1, keepdims=True),
    ]
    dot_copies = []

    def send_sums(blocks, out):
        cross = jnp.zeros((CLASSES, side), jnp.float32)
        for k, block in enumerate(blocks):
            cross = cross + block * out[k * CLASSES : (k + 1) * CLASSES]
        cross = 1.98 * jnp.sum(cross, axis=1, keepdims=True)
        line = jnp.zeros((CLASSES, 128), jnp.float32)
        for k, value in enumerate([*sums, cross]):
            line = line + jnp.where(lane == kind + k * CLASSES, value, 0.0)
        dots[0] = jnp.sum(line, axis=0, keepdims=True)
        dot_copies.append(over_clu(5, lambda o: dots.at[0], lambda k: dots_c.at[k], dots_c))

    back_m, back_c = multiply(1, from_m, from_c, send_sums)
    dot_copies[0].wait()
    line = dots[0]
    for k in range(1, n_clu):
        line = line + dots_c[k]
    dots[1] = line
    dot_copies.append(over_mem(5, lambda o: dots.at[1], lambda k: dots_m.at[k], dots_m))
    second = collect(1, back_m, back_c)
    dot_copies[1].wait()
    for k in range(1, n_mem):
        line = line + dots_m[k]
    spread_line = jnp.broadcast_to(line, (CLASSES, 128))
    bb, bq, qq, qt = [
        jnp.sum(
            jnp.where(lane == kind + k * CLASSES, spread_line, 0.0), axis=1, keepdims=True
        )
        for k in range(4)
    ]
    alpha = bb / (bb - bq)
    ratio = bq / bb
    norm = alpha * alpha * (qq - ratio * bq)
    beta = norm / bb
    h = beta - alpha * ratio
    curve = alpha * alpha * (qq - qt) + 2.0 * alpha * h * (bq - qq) + h * h * (bb - bq)
    alpha_next = norm / curve
    direction = alpha * first + h * labels
    image = alpha * (first - second) + h * (labels - first)
    scores_ref[...] = alpha * labels + alpha_next * direction
    residual_ref[...] = alpha * (first - ratio * labels) - alpha_next * image

    for copy in sent:
        copy.wait()


def finish_kernel(scores_in, residual_in, scores_out, residual_out, sems):
    copies = [
        pltpu.make_async_copy(scores_in, scores_out, sems.at[0]),
        pltpu.make_async_copy(residual_in, residual_out, sems.at[1]),
    ]
    for copy in copies:
        copy.start()
    for copy in copies:
        copy.wait()


def on_device_kernel(seed_class, seed_weight, tile_values, tile_rows, tile_cols, tile_count):
    n_clu = lax.axis_size("clu")
    n_mem = lax.axis_size("mem")
    _, _, slots, side, _ = tile_values.shape
    nodes = NB_DEV * side
    row_blocks = NB_DEV * n_mem
    col_blocks = NB_DEV * n_clu
    f32 = jnp.float32
    hbm = pl.BlockSpec(memory_space=pltpu.HBM)
    vmem = pl.BlockSpec(memory_space=pltpu.VMEM)
    dma = pltpu.SemaphoreType.DMA
    panel = (CLASSES, nodes)
    sent = (NB_DEV * CLASSES, side)
    results = (jax.ShapeDtypeStruct(panel, f32), jax.ShapeDtypeStruct(panel, f32))
    found = pl.pallas_call(
        functools.partial(solve_kernel, n_clu, n_mem),
        out_shape=results,
        in_specs=[hbm] * 6,
        out_specs=(vmem, vmem),
        scratch_shapes=[
            pltpu.VMEM((1, nodes), jnp.int32),
            pltpu.VMEM((1, nodes), f32),
            pltpu.SMEM(tile_rows.shape, jnp.int32),
            pltpu.SMEM(tile_cols.shape, jnp.int32),
            pltpu.SMEM(tile_count.shape, jnp.int32),
            pltpu.VMEM((slots, side, side), tile_values.dtype),
            pltpu.VMEM((slots, side, side), tile_values.dtype),
            pltpu.VMEM((row_blocks + 1, row_blocks, side), f32),
            pltpu.VMEM((col_blocks + 1, col_blocks, side), f32),
            pltpu.VMEM((row_blocks + 1, 2 * col_blocks - 1, CLASSES, side), f32),
            pltpu.VMEM((col_blocks + 1, 2 * row_blocks - 1, CLASSES, side), f32),
            pltpu.VMEM((n_mem + n_clu, 1, nodes), f32),
            pltpu.VMEM((n_mem, 1, nodes), f32),
            pltpu.VMEM((n_clu, 1, nodes), f32),
            pltpu.VMEM((ITERS, *sent), jnp.bfloat16),
            pltpu.VMEM((ITERS, n_mem, *sent), jnp.bfloat16),
            pltpu.VMEM((ITERS, n_clu, *sent), jnp.bfloat16),
            pltpu.VMEM((ITERS, n_mem, *panel), f32),
            pltpu.VMEM((ITERS, n_clu, *panel), f32),
            pltpu.VMEM((ITERS, n_mem, *panel), f32),
            pltpu.VMEM((ITERS, n_clu, *panel), f32),
            pltpu.VMEM((2, 1, 128), f32),
            pltpu.VMEM((n_mem, 1, 128), f32),
            pltpu.VMEM((n_clu, 1, 128), f32),
            dma((5,)),
            dma((slots // GROUP,)),
            dma((2 + 2 * ITERS,)),
            dma((2 + 2 * ITERS,)),
            dma((2 + 2 * ITERS,)),
            dma((2 + 2 * ITERS,)),
        ],
        compiler_params=pltpu.CompilerParams(
            collective_id=0, has_side_effects=True, vmem_limit_bytes=VMEM_LIMIT
        ),
        name="solve",
    )(seed_class[None], seed_weight[None], tile_values, tile_rows, tile_cols, tile_count)
    return pl.pallas_call(
        finish_kernel,
        out_shape=results,
        in_specs=[hbm, hbm],
        out_specs=(hbm, hbm),
        scratch_shapes=[dma((2,))],
        compiler_params=pltpu.CompilerParams(vmem_limit_bytes=VMEM_LIMIT),
        name="finish",
    )(*found)


def on_device(seed_class, seed_weight, tile_values, tile_rows, tile_cols, tile_count):
    side = tile_values.shape[-1]
    blocks = NB_DEV * lax.axis_size("mem") * NB_DEV * lax.axis_size("clu")
    if blocks * CLASSES * side * 16 <= TABLE_LIMIT:
        run = on_device_kernel
    else:
        run = on_device_slots
    return run(seed_class, seed_weight, tile_values, tile_rows, tile_cols, tile_count)


def solution(mesh):
    in_specs = (
        P(("clu", "mem")),
        P(("clu", "mem")),
        P("clu", "mem", None, None, None),
        P("clu", "mem", None),
        P("clu", "mem", None),
        P("clu", "mem"),
    )
    out_specs = (P(None, ("clu", "mem")), P(None, ("clu", "mem")))
    return jax.shard_map(
        on_device, mesh=mesh, in_specs=in_specs, out_specs=out_specs, check_vma=False
    )
```

```python
import functools
import jax
import jax.numpy as jnp
from jax import lax
from jax.experimental import pallas as pl
from jax.experimental.pallas import tpu as pltpu
from jax.sharding import PartitionSpec as P

CLASSES = 8
NB_DEV = 2
ITERS = 2
GROUP = 16
SPAN = 96
PACK = 4
TABLE_LIMIT = 16 * 1024 * 1024
VMEM_LIMIT = 64 * 1024 * 1024
MESH = pl.DeviceIdType.MESH


def spread(row_part, col_part):
    width = row_part.shape[0]
    from_rows = lax.psum_scatter(
        row_part.reshape(width, -1), "mem", scatter_dimension=1, tiled=True
    )
    from_cols = lax.psum_scatter(
        col_part.reshape(width, -1), "clu", scatter_dimension=1, tiled=True
    )
    return from_rows + from_cols


def squares(residual):
    return lax.psum(jnp.sum(residual * residual, axis=1), ("clu", "mem"))


def on_device_slots(seed_class, seed_weight, tile_values, tile_rows, tile_cols, tile_count):
    tiles = tile_values[0, 0]
    rows = tile_rows[0, 0]
    cols = tile_cols[0, 0]
    count = tile_count[0, 0]
    slots = tiles.shape[0]
    side = tiles.shape[1]
    row_blocks = NB_DEV * lax.axis_size("mem")
    col_blocks = NB_DEV * lax.axis_size("clu")
    valid = (jnp.arange(slots, dtype=jnp.int32) < count).astype(jnp.float32)
    row_table = (rows[None, :] == jnp.arange(row_blocks, dtype=jnp.int32)[:, None]).astype(
        jnp.float32
    ) * valid[None, :]
    col_table = (cols[None, :] == jnp.arange(col_blocks, dtype=jnp.int32)[:, None]).astype(
        jnp.float32
    ) * valid[None, :]
    highest = lax.Precision.HIGHEST
    row_totals = jnp.sum(tiles, axis=2, dtype=jnp.float32)
    col_totals = jnp.sum(tiles, axis=1, dtype=jnp.float32)
    row_part = jnp.einsum("rt,ti->ri", row_table, row_totals, precision=highest)
    col_part = jnp.einsum("kt,tj->kj", col_table, col_totals, precision=highest)
    degree = 1.0 + spread(row_part[None], col_part[None])[0]
    inverse_root = lax.rsqrt(degree)
    classes_now = jnp.arange(CLASSES, dtype=jnp.int32)[:, None]
    labels = jnp.where(seed_class[None, :] == classes_now, seed_weight[None, :], jnp.float32(0.0))
    scores = jnp.zeros_like(labels)
    residual = labels
    direction = labels
    norm_now = squares(residual)
    for step in range(ITERS):
        width = direction.shape[0]
        scaled = (inverse_root[None, :] * direction).astype(jnp.bfloat16)
        col_panel = lax.all_gather(scaled, "clu", axis=1, tiled=True).reshape(
            width, col_blocks, side
        )
        row_panel = lax.all_gather(scaled, "mem", axis=1, tiled=True).reshape(
            width, row_blocks, side
        )
        forward = jnp.einsum(
            "tij,ctj->cti",
            tiles,
            jnp.take(col_panel, cols, axis=1),
            preferred_element_type=jnp.float32,
        )
        backward = jnp.einsum(
            "tij,cti->ctj",
            tiles,
            jnp.take(row_panel, rows, axis=1),
            preferred_element_type=jnp.float32,
        )
        row_sum = jnp.einsum("rt,cti->cri", row_table, forward, precision=highest)
        col_sum = jnp.einsum("kt,ctj->ckj", col_table, backward, precision=highest)
        image_sum = spread(row_sum, col_sum)
        image = direction - 0.99 * inverse_root[None, :] * image_sum
        alpha = norm_now / lax.psum(jnp.sum(direction * image, axis=1), ("clu", "mem"))
        scores = scores + alpha[:, None] * direction
        residual = residual - alpha[:, None] * image
        if step + 1 < ITERS:
            norm_next = squares(residual)
            direction = residual + (norm_next / norm_now)[:, None] * direction
            norm_now = norm_next
    return (scores, residual)


def solve_kernel(
    n_clu,
    n_mem,
    class_hbm,
    weight_hbm,
    tiles_hbm,
    rows_hbm,
    cols_hbm,
    count_hbm,
    scores_ref,
    residual_ref,
    class_ref,
    weight_ref,
    rows_ref,
    cols_ref,
    count_ref,
    tiles,
    turned,
    hot_rows,
    hot_cols,
    from_rows,
    from_cols,
    sums_ref,
    deg_m,
    deg_c,
    own,
    pan_m,
    pan_c,
    part_m,
    part_c,
    got_m,
    got_c,
    dots,
    dots_m,
    dots_c,
    load_sems,
    tile_sems,
    send_m,
    recv_m,
    send_c,
    recv_c,
):
    me_c = lax.axis_index("clu")
    me_m = lax.axis_index("mem")
    others_m = [None] + [lax.rem(me_m + k, n_mem) for k in range(1, n_mem)]
    others_c = [None] + [lax.rem(me_c + k, n_clu) for k in range(1, n_clu)]

    slots, side, _ = tiles.shape
    row_blocks = NB_DEV * n_mem
    col_blocks = NB_DEV * n_clu
    steps = slots // GROUP

    loads = [
        pltpu.make_async_copy(rows_hbm, rows_ref, load_sems.at[0]),
        pltpu.make_async_copy(cols_hbm, cols_ref, load_sems.at[1]),
        pltpu.make_async_copy(count_hbm, count_ref, load_sems.at[2]),
        pltpu.make_async_copy(class_hbm, class_ref, load_sems.at[3]),
        pltpu.make_async_copy(weight_hbm, weight_ref, load_sems.at[4]),
    ]

    def tile_copy(g):
        part = pl.ds(g * GROUP, GROUP)
        return pltpu.make_async_copy(tiles_hbm.at[0, 0, part], tiles.at[part], tile_sems.at[g])

    for copy in loads:
        copy.start()
    for g in range(steps):
        tile_copy(g).start()
    barrier = pltpu.get_barrier_semaphore()
    for k in range(1, n_mem):
        pl.semaphore_signal(barrier, device_id=(me_c, others_m[k]), device_id_type=MESH)
    for k in range(1, n_clu):
        pl.semaphore_signal(barrier, device_id=(others_c[k], me_m), device_id_type=MESH)

    sent = []

    def whole(room, count, send_sem, recv_sem):
        view = room.at[pl.ds(0, count - 1)]
        sent.append(pltpu.make_async_copy(view, view, send_sem))
        return pltpu.make_async_copy(view, view, recv_sem)

    def over_mem(phase, source, target, room):
        for k in range(1, n_mem):
            pltpu.make_async_remote_copy(
                src_ref=source(others_m[k]),
                dst_ref=target(k),
                send_sem=send_m.at[phase],
                recv_sem=recv_m.at[phase],
                device_id=(me_c, others_m[k]),
                device_id_type=MESH,
            ).start()
        return whole(room, n_mem, send_m.at[phase], recv_m.at[phase])

    def over_clu(phase, source, target, room):
        for k in range(1, n_clu):
            pltpu.make_async_remote_copy(
                src_ref=source(others_c[k]),
                dst_ref=target(k),
                send_sem=send_c.at[phase],
                recv_sem=recv_c.at[phase],
                device_id=(others_c[k], me_m),
                device_id_type=MESH,
            ).start()
        return whole(room, n_clu, send_c.at[phase], recv_c.at[phase])

    for copy in loads:
        copy.wait()
    count = count_ref[0, 0]
    kinds = lax.broadcasted_iota(jnp.int32, (CLASSES, weight_ref.shape[1]), 0)
    labels = jnp.where(class_ref[...] == kinds, weight_ref[...], jnp.float32(0.0))

    for blocks, hot in ((row_blocks, hot_rows), (col_blocks, hot_cols)):
        at = lax.broadcasted_iota(jnp.int32, (blocks, side), 0)
        for k in range(blocks + 1):
            hot[k] = jnp.where(at == k, jnp.float32(1.0), jnp.float32(0.0))
    from_rows[...] = jnp.zeros_like(from_rows)
    from_cols[...] = jnp.zeros_like(from_cols)

    def used(slot, block, blocks):
        unused = 1 - jnp.clip(count - slot, 0, 1)
        return block + (blocks - block) * unused

    def dot(left, held, slot):
        right = held[pl.ds(slot, PACK)].reshape(PACK * side, side)
        return lax.dot_general(
            jnp.concatenate(left, axis=1),
            right,
            (((1,), (0,)), ((), ())),
            preferred_element_type=jnp.float32,
        )

    def blocks_used(first, count, own_ref, own_blocks, hot):
        return [
            hot[used(slot, own_ref[0, 0, slot], own_blocks)].astype(jnp.bfloat16)
            for slot in range(first, first + count)
        ]

    total = jnp.zeros((row_blocks, side), jnp.float32)
    for g in range(steps):
        tile_copy(g).wait()
        for first in range(g * GROUP, (g + 1) * GROUP, 2):
            pair = lax.dot_general(
                jnp.concatenate(blocks_used(first, 2, rows_ref, row_blocks, hot_rows), axis=0),
                tiles[pl.ds(first, 2)].reshape(2 * side, side),
                (((1,), (1,)), ((), ())),
                preferred_element_type=jnp.float32,
            )
            total = total + pair[:row_blocks, :side] + pair[row_blocks:, side:]
    for k in range(row_blocks):
        at = k % NB_DEV * side
        sums_ref[k // NB_DEV, :, at : at + side] = total[k : k + 1]
    pl.semaphore_wait(barrier, n_mem + n_clu - 2)
    from_m = over_mem(0, lambda o: sums_ref.at[o], lambda k: deg_m.at[k], deg_m)

    total = jnp.zeros((col_blocks, side), jnp.float32)
    for first in range(0, slots, PACK):
        total = total + dot(blocks_used(first, PACK, cols_ref, col_blocks, hot_cols), tiles, first)
    for k in range(col_blocks):
        at = k % NB_DEV * side
        sums_ref[n_mem + k // NB_DEV, :, at : at + side] = total[k : k + 1]
    from_c = over_clu(0, lambda o: sums_ref.at[n_mem + o], lambda k: deg_c.at[k], deg_c)

    def turn(g, carry):
        for slot in [g * GROUP + k for k in range(GROUP)]:
            turned[slot] = tiles[slot].T
        return carry

    def place_sums(table, held, own_ref, own_blocks, to_ref, to_blocks):
        def step(g, total):
            for k in range(0, SPAN, PACK):
                left = []
                for slot in [g * SPAN + k + e for e in range(PACK)]:
                    block = used(slot, own_ref[0, 0, slot], own_blocks)
                    start = to_blocks - 1 - to_ref[0, 0, slot]
                    panel = table[block, pl.ds(start, to_blocks)]
                    left.append(panel.reshape(to_blocks * CLASSES, side).astype(jnp.bfloat16))
                total = total + dot(left, held, g * SPAN + k)
            return total

        zero = jnp.zeros((to_blocks * CLASSES, side), jnp.float32)
        return lax.fori_loop(0, slots // SPAN, step, zero)

    def column_sums():
        return place_sums(from_rows, tiles, rows_ref, row_blocks, cols_ref, col_blocks)

    def row_sums():
        return place_sums(from_cols, turned, cols_ref, col_blocks, rows_ref, row_blocks)

    lax.fori_loop(0, steps // 2, turn, 0)
    degree = 1.0 + (sums_ref[me_m] + sums_ref[n_mem + me_c])
    from_m.wait()
    for k in range(1, n_mem):
        degree = degree + deg_m[k]
    from_c.wait()
    for k in range(1, n_clu):
        degree = degree + deg_c[k]
    root = lax.rsqrt(degree)

    def gather(step, panel):
        panel = jnp.concatenate(
            [panel[:, k * side : (k + 1) * side] for k in range(NB_DEV)], axis=0
        ).astype(jnp.bfloat16)
        own[step] = panel
        pan_m[step, me_m] = panel
        pan_c[step, me_c] = panel
        from_m = over_mem(1 + 2 * step, lambda o: own.at[step], lambda k: pan_m.at[step, me_m], pan_m.at[step])
        from_c = over_clu(1 + 2 * step, lambda o: own.at[step], lambda k: pan_c.at[step, me_c], pan_c.at[step])
        return from_m, from_c

    def place_panels(panels, count, table, at):
        blocks = []
        for k in range(count):
            panel = panels[k].astype(jnp.float32).reshape(NB_DEV, CLASSES, side)
            for e in range(NB_DEV):
                blocks.append(panel[e])
                table[k * NB_DEV + e, at] = panel[e]
        return blocks

    def parts_of(out, parts, blocks):
        for k in range(blocks):
            at = k % NB_DEV * side
            parts[k // NB_DEV, :, at : at + side] = out[k * CLASSES : (k + 1) * CLASSES]

    def multiply(step, from_m, from_c, between):
        phase = 2 + 2 * step
        from_c.wait()
        place_panels(pan_c.at[step], n_clu, from_cols, row_blocks - 1)
        out = row_sums()
        parts_of(out, part_m.at[step], row_blocks)
        back_m = over_mem(
            phase, lambda o: part_m.at[step, o], lambda k: got_m.at[step, k], got_m.at[step]
        )
        from_m.wait()
        between(place_panels(pan_m.at[step], n_mem, from_rows, col_blocks - 1), out)
        parts_of(column_sums(), part_c.at[step], col_blocks)
        back_c = over_clu(
            phase, lambda o: part_c.at[step, o], lambda k: got_c.at[step, k], got_c.at[step]
        )
        return back_m, back_c

    def collect(step, back_m, back_c):
        image = part_m[step, me_m] + part_c[step, me_c]
        back_m.wait()
        for k in range(1, n_mem):
            image = image + got_m[step, k]
        back_c.wait()
        for k in range(1, n_clu):
            image = image + got_c[step, k]
        return 0.99 * root * image

    from_m, from_c = gather(0, root * labels)
    lax.fori_loop(steps // 2, steps, turn, 0)
    back_m, back_c = multiply(0, from_m, from_c, lambda blocks, out: None)
    first = collect(0, back_m, back_c)

    from_m, from_c = gather(1, root * first)
    lane = lax.broadcasted_iota(jnp.int32, (CLASSES, 128), 1)
    kind = lax.broadcasted_iota(jnp.int32, (CLASSES, 128), 0)
    sums = [
        jnp.sum(labels * labels, axis=1, keepdims=True),
        jnp.sum(labels * first, axis=1, keepdims=True),
        jnp.sum(first * first, axis=1, keepdims=True),
    ]
    dot_copies = []

    def send_sums(blocks, out):
        cross = jnp.zeros((CLASSES, side), jnp.float32)
        for k, block in enumerate(blocks):
            cross = cross + block * out[k * CLASSES : (k + 1) * CLASSES]
        cross = 1.98 * jnp.sum(cross, axis=1, keepdims=True)
        line = jnp.zeros((CLASSES, 128), jnp.float32)
        for k, value in enumerate([*sums, cross]):
            line = line + jnp.where(lane == kind + k * CLASSES, value, 0.0)
        dots[0] = jnp.sum(line, axis=0, keepdims=True)
        dot_copies.append(over_clu(5, lambda o: dots.at[0], lambda k: dots_c.at[k], dots_c))

    back_m, back_c = multiply(1, from_m, from_c, send_sums)
    dot_copies[0].wait()
    line = dots[0]
    for k in range(1, n_clu):
        line = line + dots_c[k]
    dots[1] = line
    dot_copies.append(over_mem(5, lambda o: dots.at[1], lambda k: dots_m.at[k], dots_m))
    second = collect(1, back_m, back_c)
    dot_copies[1].wait()
    for k in range(1, n_mem):
        line = line + dots_m[k]
    spread_line = jnp.broadcast_to(line, (CLASSES, 128))
    bb, bq, qq, qt = [
        jnp.sum(
            jnp.where(lane == kind + k * CLASSES, spread_line, 0.0), axis=1, keepdims=True
        )
        for k in range(4)
    ]
    alpha = bb / (bb - bq)
    ratio = bq / bb
    norm = alpha * alpha * (qq - ratio * bq)
    beta = norm / bb
    h = beta - alpha * ratio
    curve = alpha * alpha * (qq - qt) + 2.0 * alpha * h * (bq - qq) + h * h * (bb - bq)
    alpha_next = norm / curve
    direction = alpha * first + h * labels
    image = alpha * (first - second) + h * (labels - first)
    scores_ref[...] = alpha * labels + alpha_next * direction
    residual_ref[...] = alpha * (first - ratio * labels) - alpha_next * image

    for copy in sent:
        copy.wait()


def finish_kernel(scores_in, residual_in, scores_out, residual_out, sems):
    copies = [
        pltpu.make_async_copy(scores_in, scores_out, sems.at[0]),
        pltpu.make_async_copy(residual_in, residual_out, sems.at[1]),
    ]
    for copy in copies:
        copy.start()
    for copy in copies:
        copy.wait()


def on_device_kernel(seed_class, seed_weight, tile_values, tile_rows, tile_cols, tile_count):
    n_clu = lax.axis_size("clu")
    n_mem = lax.axis_size("mem")
    _, _, slots, side, _ = tile_values.shape
    nodes = NB_DEV * side
    row_blocks = NB_DEV * n_mem
    col_blocks = NB_DEV * n_clu
    f32 = jnp.float32
    hbm = pl.BlockSpec(memory_space=pltpu.HBM)
    vmem = pl.BlockSpec(memory_space=pltpu.VMEM)
    dma = pltpu.SemaphoreType.DMA
    panel = (CLASSES, nodes)
    sent = (NB_DEV * CLASSES, side)
    results = (jax.ShapeDtypeStruct(panel, f32), jax.ShapeDtypeStruct(panel, f32))
    found = pl.pallas_call(
        functools.partial(solve_kernel, n_clu, n_mem),
        out_shape=results,
        in_specs=[hbm] * 6,
        out_specs=(vmem, vmem),
        scratch_shapes=[
            pltpu.VMEM((1, nodes), jnp.int32),
            pltpu.VMEM((1, nodes), f32),
            pltpu.SMEM(tile_rows.shape, jnp.int32),
            pltpu.SMEM(tile_cols.shape, jnp.int32),
            pltpu.SMEM(tile_count.shape, jnp.int32),
            pltpu.VMEM((slots, side, side), tile_values.dtype),
            pltpu.VMEM((slots, side, side), tile_values.dtype),
            pltpu.VMEM((row_blocks + 1, row_blocks, side), f32),
            pltpu.VMEM((col_blocks + 1, col_blocks, side), f32),
            pltpu.VMEM((row_blocks + 1, 2 * col_blocks - 1, CLASSES, side), f32),
            pltpu.VMEM((col_blocks + 1, 2 * row_blocks - 1, CLASSES, side), f32),
            pltpu.VMEM((n_mem + n_clu, 1, nodes), f32),
            pltpu.VMEM((n_mem, 1, nodes), f32),
            pltpu.VMEM((n_clu, 1, nodes), f32),
            pltpu.VMEM((ITERS, *sent), jnp.bfloat16),
            pltpu.VMEM((ITERS, n_mem, *sent), jnp.bfloat16),
            pltpu.VMEM((ITERS, n_clu, *sent), jnp.bfloat16),
            pltpu.VMEM((ITERS, n_mem, *panel), f32),
            pltpu.VMEM((ITERS, n_clu, *panel), f32),
            pltpu.VMEM((ITERS, n_mem, *panel), f32),
            pltpu.VMEM((ITERS, n_clu, *panel), f32),
            pltpu.VMEM((2, 1, 128), f32),
            pltpu.VMEM((n_mem, 1, 128), f32),
            pltpu.VMEM((n_clu, 1, 128), f32),
            dma((5,)),
            dma((slots // GROUP,)),
            dma((2 + 2 * ITERS,)),
            dma((2 + 2 * ITERS,)),
            dma((2 + 2 * ITERS,)),
            dma((2 + 2 * ITERS,)),
        ],
        compiler_params=pltpu.CompilerParams(
            collective_id=0, has_side_effects=True, vmem_limit_bytes=VMEM_LIMIT
        ),
        name="solve",
    )(seed_class[None], seed_weight[None], tile_values, tile_rows, tile_cols, tile_count)
    return pl.pallas_call(
        finish_kernel,
        out_shape=results,
        in_specs=[hbm, hbm],
        out_specs=(hbm, hbm),
        scratch_shapes=[dma((2,))],
        compiler_params=pltpu.CompilerParams(vmem_limit_bytes=VMEM_LIMIT),
        name="finish",
    )(*found)


def on_device(seed_class, seed_weight, tile_values, tile_rows, tile_cols, tile_count):
    side = tile_values.shape[-1]
    blocks = NB_DEV * lax.axis_size("mem") * NB_DEV * lax.axis_size("clu")
    if blocks * CLASSES * side * 16 <= TABLE_LIMIT:
        run = on_device_kernel
    else:
        run = on_device_slots
    return run(seed_class, seed_weight, tile_values, tile_rows, tile_cols, tile_count)


def solution(mesh):
    in_specs = (
        P(("clu", "mem")),
        P(("clu", "mem")),
        P("clu", "mem", None, None, None),
        P("clu", "mem", None),
        P("clu", "mem", None),
        P("clu", "mem"),
    )
    out_specs = (P(None, ("clu", "mem")), P(None, ("clu", "mem")))
    return jax.shard_map(
        on_device, mesh=mesh, in_specs=in_specs, out_specs=out_specs, check_vma=False
    )
```

```python
import functools
import jax
import jax.numpy as jnp
from jax import lax
from jax.experimental import pallas as pl
from jax.experimental.pallas import tpu as pltpu
from jax.sharding import PartitionSpec as P

CLASSES = 8
NB_DEV = 2
ITERS = 2
GROUP = 16
SPAN = 96
PACK = 4
TABLE_LIMIT = 16 * 1024 * 1024
VMEM_LIMIT = 64 * 1024 * 1024
MESH = pl.DeviceIdType.MESH


def spread(row_part, col_part):
    width = row_part.shape[0]
    from_rows = lax.psum_scatter(
        row_part.reshape(width, -1), "mem", scatter_dimension=1, tiled=True
    )
    from_cols = lax.psum_scatter(
        col_part.reshape(width, -1), "clu", scatter_dimension=1, tiled=True
    )
    return from_rows + from_cols


def squares(residual):
    return lax.psum(jnp.sum(residual * residual, axis=1), ("clu", "mem"))


def on_device_slots(seed_class, seed_weight, tile_values, tile_rows, tile_cols, tile_count):
    tiles = tile_values[0, 0]
    rows = tile_rows[0, 0]
    cols = tile_cols[0, 0]
    count = tile_count[0, 0]
    slots = tiles.shape[0]
    side = tiles.shape[1]
    row_blocks = NB_DEV * lax.axis_size("mem")
    col_blocks = NB_DEV * lax.axis_size("clu")
    valid = (jnp.arange(slots, dtype=jnp.int32) < count).astype(jnp.float32)
    row_table = (rows[None, :] == jnp.arange(row_blocks, dtype=jnp.int32)[:, None]).astype(
        jnp.float32
    ) * valid[None, :]
    col_table = (cols[None, :] == jnp.arange(col_blocks, dtype=jnp.int32)[:, None]).astype(
        jnp.float32
    ) * valid[None, :]
    highest = lax.Precision.HIGHEST
    row_totals = jnp.sum(tiles, axis=2, dtype=jnp.float32)
    col_totals = jnp.sum(tiles, axis=1, dtype=jnp.float32)
    row_part = jnp.einsum("rt,ti->ri", row_table, row_totals, precision=highest)
    col_part = jnp.einsum("kt,tj->kj", col_table, col_totals, precision=highest)
    degree = 1.0 + spread(row_part[None], col_part[None])[0]
    inverse_root = lax.rsqrt(degree)
    classes_now = jnp.arange(CLASSES, dtype=jnp.int32)[:, None]
    labels = jnp.where(seed_class[None, :] == classes_now, seed_weight[None, :], jnp.float32(0.0))
    scores = jnp.zeros_like(labels)
    residual = labels
    direction = labels
    norm_now = squares(residual)
    for step in range(ITERS):
        width = direction.shape[0]
        scaled = (inverse_root[None, :] * direction).astype(jnp.bfloat16)
        col_panel = lax.all_gather(scaled, "clu", axis=1, tiled=True).reshape(
            width, col_blocks, side
        )
        row_panel = lax.all_gather(scaled, "mem", axis=1, tiled=True).reshape(
            width, row_blocks, side
        )
        forward = jnp.einsum(
            "tij,ctj->cti",
            tiles,
            jnp.take(col_panel, cols, axis=1),
            preferred_element_type=jnp.float32,
        )
        backward = jnp.einsum(
            "tij,cti->ctj",
            tiles,
            jnp.take(row_panel, rows, axis=1),
            preferred_element_type=jnp.float32,
        )
        row_sum = jnp.einsum("rt,cti->cri", row_table, forward, precision=highest)
        col_sum = jnp.einsum("kt,ctj->ckj", col_table, backward, precision=highest)
        image_sum = spread(row_sum, col_sum)
        image = direction - 0.99 * inverse_root[None, :] * image_sum
        alpha = norm_now / lax.psum(jnp.sum(direction * image, axis=1), ("clu", "mem"))
        scores = scores + alpha[:, None] * direction
        residual = residual - alpha[:, None] * image
        if step + 1 < ITERS:
            norm_next = squares(residual)
            direction = residual + (norm_next / norm_now)[:, None] * direction
            norm_now = norm_next
    return (scores, residual)


def solve_kernel(
    n_clu,
    n_mem,
    class_hbm,
    weight_hbm,
    tiles_hbm,
    rows_hbm,
    cols_hbm,
    count_hbm,
    scores_hbm,
    residual_hbm,
    scores_ref,
    residual_ref,
    class_ref,
    weight_ref,
    rows_ref,
    cols_ref,
    count_ref,
    places,
    tiles,
    turned,
    hot_rows,
    hot_cols,
    from_rows,
    from_cols,
    sums_ref,
    deg_m,
    deg_c,
    own,
    pan_m,
    pan_c,
    part_m,
    part_c,
    got_m,
    got_c,
    dots,
    dots_m,
    dots_c,
    load_sems,
    out_sems,
    tile_sems,
    send_m,
    recv_m,
    send_c,
    recv_c,
):
    me_c = lax.axis_index("clu")
    me_m = lax.axis_index("mem")
    others_m = [None] + [lax.rem(me_m + k, n_mem) for k in range(1, n_mem)]
    others_c = [None] + [lax.rem(me_c + k, n_clu) for k in range(1, n_clu)]

    slots, side, _ = tiles.shape
    row_blocks = NB_DEV * n_mem
    col_blocks = NB_DEV * n_clu
    steps = slots // GROUP

    loads = [
        pltpu.make_async_copy(rows_hbm, rows_ref, load_sems.at[0]),
        pltpu.make_async_copy(cols_hbm, cols_ref, load_sems.at[1]),
        pltpu.make_async_copy(count_hbm, count_ref, load_sems.at[2]),
        pltpu.make_async_copy(class_hbm, class_ref, load_sems.at[3]),
        pltpu.make_async_copy(weight_hbm, weight_ref, load_sems.at[4]),
    ]

    def tile_copy(g):
        part = pl.ds(g * GROUP, GROUP)
        return pltpu.make_async_copy(tiles_hbm.at[0, 0, part], tiles.at[part], tile_sems.at[g])

    for copy in loads:
        copy.start()
    for g in range(steps):
        tile_copy(g).start()
    barrier = pltpu.get_barrier_semaphore()
    for k in range(1, n_mem):
        pl.semaphore_signal(barrier, device_id=(me_c, others_m[k]), device_id_type=MESH)
    for k in range(1, n_clu):
        pl.semaphore_signal(barrier, device_id=(others_c[k], me_m), device_id_type=MESH)

    sent = []

    def whole(room, count, send_sem, recv_sem):
        view = room.at[pl.ds(0, count - 1)]
        sent.append(pltpu.make_async_copy(view, view, send_sem))
        return pltpu.make_async_copy(view, view, recv_sem)

    def over_mem(phase, source, target, room):
        for k in range(1, n_mem):
            pltpu.make_async_remote_copy(
                src_ref=source(others_m[k]),
                dst_ref=target(k),
                send_sem=send_m.at[phase],
                recv_sem=recv_m.at[phase],
                device_id=(me_c, others_m[k]),
                device_id_type=MESH,
            ).start()
        return whole(room, n_mem, send_m.at[phase], recv_m.at[phase])

    def over_clu(phase, source, target, room):
        for k in range(1, n_clu):
            pltpu.make_async_remote_copy(
                src_ref=source(others_c[k]),
                dst_ref=target(k),
                send_sem=send_c.at[phase],
                recv_sem=recv_c.at[phase],
                device_id=(others_c[k], me_m),
                device_id_type=MESH,
            ).start()
        return whole(room, n_clu, send_c.at[phase], recv_c.at[phase])

    for copy in loads:
        copy.wait()
    count = count_ref[0, 0]
    kinds = lax.broadcasted_iota(jnp.int32, (CLASSES, weight_ref.shape[1]), 0)
    labels = jnp.where(class_ref[...] == kinds, weight_ref[...], jnp.float32(0.0))

    for blocks, hot in ((row_blocks, hot_rows), (col_blocks, hot_cols)):
        at = lax.broadcasted_iota(jnp.int32, (blocks, side), 0)
        for k in range(blocks + 1):
            hot[k] = jnp.where(at == k, jnp.float32(1.0), jnp.float32(0.0))
    from_rows[...] = jnp.zeros_like(from_rows)
    from_cols[...] = jnp.zeros_like(from_cols)

    def used(slot, block, blocks):
        unused = 1 - jnp.clip(count - slot, 0, 1)
        return block + (blocks - block) * unused

    def dot(left, held, slot):
        right = held[pl.ds(slot, PACK)].reshape(PACK * side, side)
        return lax.dot_general(
            jnp.concatenate(left, axis=1),
            right,
            (((1,), (0,)), ((), ())),
            preferred_element_type=jnp.float32,
        )

    def blocks_used(first, count, own_ref, own_blocks, hot, side_at, to_ref, to_blocks):
        blocks = []
        for slot in range(first, first + count):
            block = used(slot, own_ref[0, 0, slot], own_blocks)
            start = to_blocks - 1 - to_ref[0, 0, slot]
            places[side_at, slot] = block * (2 * to_blocks - 1) + start
            blocks.append(hot[block].astype(jnp.bfloat16))
        return blocks

    total = jnp.zeros((row_blocks, side), jnp.float32)
    for g in range(steps):
        tile_copy(g).wait()
        for first in range(g * GROUP, (g + 1) * GROUP, 2):
            pair = lax.dot_general(
                jnp.concatenate(
                    blocks_used(
                        first, 2, rows_ref, row_blocks, hot_rows, 0, cols_ref, col_blocks
                    ),
                    axis=0,
                ),
                tiles[pl.ds(first, 2)].reshape(2 * side, side),
                (((1,), (1,)), ((), ())),
                preferred_element_type=jnp.float32,
            )
            total = total + pair[:row_blocks, :side] + pair[row_blocks:, side:]
    for k in range(row_blocks):
        at = k % NB_DEV * side
        sums_ref[k // NB_DEV, :, at : at + side] = total[k : k + 1]
    pl.semaphore_wait(barrier, n_mem + n_clu - 2)
    from_m = over_mem(0, lambda o: sums_ref.at[o], lambda k: deg_m.at[k], deg_m)

    total = jnp.zeros((col_blocks, side), jnp.float32)
    for first in range(0, slots, PACK):
        left = blocks_used(
            first, PACK, cols_ref, col_blocks, hot_cols, 1, rows_ref, row_blocks
        )
        total = total + dot(left, tiles, first)
    for k in range(col_blocks):
        at = k % NB_DEV * side
        sums_ref[n_mem + k // NB_DEV, :, at : at + side] = total[k : k + 1]
    from_c = over_clu(0, lambda o: sums_ref.at[n_mem + o], lambda k: deg_c.at[k], deg_c)

    def turn(g, carry):
        for slot in [g * GROUP + k for k in range(GROUP)]:
            turned[slot] = tiles[slot].T
        return carry

    def place_sums(table, held, side_at, to_blocks):
        def step(g, total):
            for k in range(0, SPAN, PACK):
                left = []
                for slot in [g * SPAN + k + e for e in range(PACK)]:
                    panel = table[pl.ds(places[side_at, slot], to_blocks)]
                    left.append(panel.reshape(to_blocks * CLASSES, side).astype(jnp.bfloat16))
                total = total + dot(left, held, g * SPAN + k)
            return total

        zero = jnp.zeros((to_blocks * CLASSES, side), jnp.float32)
        return lax.fori_loop(0, slots // SPAN, step, zero)

    def column_sums():
        return place_sums(from_rows, tiles, 0, col_blocks)

    def row_sums():
        return place_sums(from_cols, turned, 1, row_blocks)

    lax.fori_loop(0, steps // 2, turn, 0)
    degree = 1.0 + (sums_ref[me_m] + sums_ref[n_mem + me_c])
    from_m.wait()
    for k in range(1, n_mem):
        degree = degree + deg_m[k]
    from_c.wait()
    for k in range(1, n_clu):
        degree = degree + deg_c[k]
    root = lax.rsqrt(degree)

    def gather(step, panel):
        panel = jnp.concatenate(
            [panel[:, k * side : (k + 1) * side] for k in range(NB_DEV)], axis=0
        ).astype(jnp.bfloat16)
        own[step] = panel
        pan_m[step, me_m] = panel
        pan_c[step, me_c] = panel
        from_m = over_mem(1 + 2 * step, lambda o: own.at[step], lambda k: pan_m.at[step, me_m], pan_m.at[step])
        from_c = over_clu(1 + 2 * step, lambda o: own.at[step], lambda k: pan_c.at[step, me_c], pan_c.at[step])
        return from_m, from_c

    def place_panels(panels, count, table, to_blocks):
        blocks = []
        for k in range(count):
            panel = panels[k].astype(jnp.float32).reshape(NB_DEV, CLASSES, side)
            for e in range(NB_DEV):
                blocks.append(panel[e])
                table[(k * NB_DEV + e) * (2 * to_blocks - 1) + to_blocks - 1] = panel[e]
        return blocks

    def parts_of(out, parts, blocks):
        for k in range(blocks):
            at = k % NB_DEV * side
            parts[k // NB_DEV, :, at : at + side] = out[k * CLASSES : (k + 1) * CLASSES]

    def multiply(step, from_m, from_c, between):
        phase = 2 + 2 * step
        from_c.wait()
        place_panels(pan_c.at[step], n_clu, from_cols, row_blocks)
        out = row_sums()
        parts_of(out, part_m.at[step], row_blocks)
        back_m = over_mem(
            phase, lambda o: part_m.at[step, o], lambda k: got_m.at[step, k], got_m.at[step]
        )
        from_m.wait()
        between(place_panels(pan_m.at[step], n_mem, from_rows, col_blocks), out)
        parts_of(column_sums(), part_c.at[step], col_blocks)
        back_c = over_clu(
            phase, lambda o: part_c.at[step, o], lambda k: got_c.at[step, k], got_c.at[step]
        )
        return back_m, back_c

    def collect(step, back_m, back_c):
        image = part_m[step, me_m] + part_c[step, me_c]
        back_m.wait()
        for k in range(1, n_mem):
            image = image + got_m[step, k]
        back_c.wait()
        for k in range(1, n_clu):
            image = image + got_c[step, k]
        return 0.99 * root * image

    from_m, from_c = gather(0, root * labels)
    lax.fori_loop(steps // 2, steps, turn, 0)
    back_m, back_c = multiply(0, from_m, from_c, lambda blocks, out: None)
    first = collect(0, back_m, back_c)

    from_m, from_c = gather(1, root * first)
    lane = lax.broadcasted_iota(jnp.int32, (CLASSES, 128), 1)
    kind = lax.broadcasted_iota(jnp.int32, (CLASSES, 128), 0)
    sums = [
        jnp.sum(labels * labels, axis=1, keepdims=True),
        jnp.sum(labels * first, axis=1, keepdims=True),
        jnp.sum(first * first, axis=1, keepdims=True),
    ]
    dot_copies = []

    def send_sums(blocks, out):
        cross = jnp.zeros((CLASSES, side), jnp.float32)
        for k, block in enumerate(blocks):
            cross = cross + block * out[k * CLASSES : (k + 1) * CLASSES]
        cross = 1.98 * jnp.sum(cross, axis=1, keepdims=True)
        line = jnp.zeros((CLASSES, 128), jnp.float32)
        for k, value in enumerate([*sums, cross]):
            line = line + jnp.where(lane == kind + k * CLASSES, value, 0.0)
        dots[0] = jnp.sum(line, axis=0, keepdims=True)
        dot_copies.append(over_clu(5, lambda o: dots.at[0], lambda k: dots_c.at[k], dots_c))

    back_m, back_c = multiply(1, from_m, from_c, send_sums)
    dot_copies[0].wait()
    line = dots[0]
    for k in range(1, n_clu):
        line = line + dots_c[k]
    dots[1] = line
    dot_copies.append(over_mem(5, lambda o: dots.at[1], lambda k: dots_m.at[k], dots_m))
    second = collect(1, back_m, back_c)
    dot_copies[1].wait()
    for k in range(1, n_mem):
        line = line + dots_m[k]
    spread_line = jnp.broadcast_to(line, (CLASSES, 128))
    bb, bq, qq, qt = [
        jnp.sum(
            jnp.where(lane == kind + k * CLASSES, spread_line, 0.0), axis=1, keepdims=True
        )
        for k in range(4)
    ]
    alpha = bb / (bb - bq)
    ratio = bq / bb
    norm = alpha * alpha * (qq - ratio * bq)
    beta = norm / bb
    h = beta - alpha * ratio
    curve = alpha * alpha * (qq - qt) + 2.0 * alpha * h * (bq - qq) + h * h * (bb - bq)
    alpha_next = norm / curve
    direction = alpha * first + h * labels
    image = alpha * (first - second) + h * (labels - first)
    scores_ref[...] = alpha * labels + alpha_next * direction
    residual_ref[...] = alpha * (first - ratio * labels) - alpha_next * image

    results = [
        pltpu.make_async_copy(scores_ref, scores_hbm, out_sems.at[0]),
        pltpu.make_async_copy(residual_ref, residual_hbm, out_sems.at[1]),
    ]
    for copy in results:
        copy.start()
    for copy in sent + results:
        copy.wait()


def finish_kernel(scores_in, residual_in, scores_out, residual_out, sems):
    copies = [
        pltpu.make_async_copy(scores_in, scores_out, sems.at[0]),
        pltpu.make_async_copy(residual_in, residual_out, sems.at[1]),
    ]
    for copy in copies:
        copy.start()
    for copy in copies:
        copy.wait()


def on_device_kernel(seed_class, seed_weight, tile_values, tile_rows, tile_cols, tile_count):
    n_clu = lax.axis_size("clu")
    n_mem = lax.axis_size("mem")
    _, _, slots, side, _ = tile_values.shape
    nodes = NB_DEV * side
    row_blocks = NB_DEV * n_mem
    col_blocks = NB_DEV * n_clu
    f32 = jnp.float32
    hbm = pl.BlockSpec(memory_space=pltpu.HBM)
    dma = pltpu.SemaphoreType.DMA
    panel = (CLASSES, nodes)
    sent = (NB_DEV * CLASSES, side)
    results = (jax.ShapeDtypeStruct(panel, f32), jax.ShapeDtypeStruct(panel, f32))
    found = pl.pallas_call(
        functools.partial(solve_kernel, n_clu, n_mem),
        out_shape=results,
        in_specs=[hbm] * 6,
        out_specs=(hbm, hbm),
        scratch_shapes=[
            pltpu.VMEM(panel, f32),
            pltpu.VMEM(panel, f32),
            pltpu.VMEM((1, nodes), jnp.int32),
            pltpu.VMEM((1, nodes), f32),
            pltpu.SMEM(tile_rows.shape, jnp.int32),
            pltpu.SMEM(tile_cols.shape, jnp.int32),
            pltpu.SMEM(tile_count.shape, jnp.int32),
            pltpu.SMEM((2, slots), jnp.int32),
            pltpu.VMEM((slots, side, side), tile_values.dtype),
            pltpu.VMEM((slots, side, side), tile_values.dtype),
            pltpu.VMEM((row_blocks + 1, row_blocks, side), f32),
            pltpu.VMEM((col_blocks + 1, col_blocks, side), f32),
            pltpu.VMEM(((row_blocks + 1) * (2 * col_blocks - 1), CLASSES, side), f32),
            pltpu.VMEM(((col_blocks + 1) * (2 * row_blocks - 1), CLASSES, side), f32),
            pltpu.VMEM((n_mem + n_clu, 1, nodes), f32),
            pltpu.VMEM((n_mem, 1, nodes), f32),
            pltpu.VMEM((n_clu, 1, nodes), f32),
            pltpu.VMEM((ITERS, *sent), jnp.bfloat16),
            pltpu.VMEM((ITERS, n_mem, *sent), jnp.bfloat16),
            pltpu.VMEM((ITERS, n_clu, *sent), jnp.bfloat16),
            pltpu.VMEM((ITERS, n_mem, *panel), f32),
            pltpu.VMEM((ITERS, n_clu, *panel), f32),
            pltpu.VMEM((ITERS, n_mem, *panel), f32),
            pltpu.VMEM((ITERS, n_clu, *panel), f32),
            pltpu.VMEM((2, 1, 128), f32),
            pltpu.VMEM((n_mem, 1, 128), f32),
            pltpu.VMEM((n_clu, 1, 128), f32),
            dma((5,)),
            dma((2,)),
            dma((slots // GROUP,)),
            dma((2 + 2 * ITERS,)),
            dma((2 + 2 * ITERS,)),
            dma((2 + 2 * ITERS,)),
            dma((2 + 2 * ITERS,)),
        ],
        compiler_params=pltpu.CompilerParams(
            collective_id=0, has_side_effects=True, vmem_limit_bytes=VMEM_LIMIT
        ),
        name="solve",
    )(seed_class[None], seed_weight[None], tile_values, tile_rows, tile_cols, tile_count)
    return pl.pallas_call(
        finish_kernel,
        out_shape=results,
        in_specs=[hbm, hbm],
        out_specs=(hbm, hbm),
        scratch_shapes=[dma((2,))],
        compiler_params=pltpu.CompilerParams(vmem_limit_bytes=VMEM_LIMIT),
        name="finish",
    )(*found)


def on_device(seed_class, seed_weight, tile_values, tile_rows, tile_cols, tile_count):
    side = tile_values.shape[-1]
    blocks = NB_DEV * lax.axis_size("mem") * NB_DEV * lax.axis_size("clu")
    if blocks * CLASSES * side * 16 <= TABLE_LIMIT:
        run = on_device_kernel
    else:
        run = on_device_slots
    return run(seed_class, seed_weight, tile_values, tile_rows, tile_cols, tile_count)


def solution(mesh):
    in_specs = (
        P(("clu", "mem")),
        P(("clu", "mem")),
        P("clu", "mem", None, None, None),
        P("clu", "mem", None),
        P("clu", "mem", None),
        P("clu", "mem"),
    )
    out_specs = (P(None, ("clu", "mem")), P(None, ("clu", "mem")))
    return jax.shard_map(
        on_device, mesh=mesh, in_specs=in_specs, out_specs=out_specs, check_vma=False
    )
```
